256 devices in a mesh: dp: 32 (over x, y, core), mp: 8 (over z).
Axes of the slice: x: 4, y: 4, z: 8, core: 2. Of those that a mesh axis runs over, the one named last changes fastest.
Arguments:
- inputs: bfloat16 [24576, 4096], P('dp'), may hold values from -6 to 6
- query_grad: bfloat16 [24576, 4096], P('dp', 'mp'), may hold values from -6 to 6
- master_weight: float32 [4096, 4096], P('dp', 'mp'), may hold values from -24 to 24
- row_factor: float32 [4096], P('dp'), may hold values from 0 to 1, as said below
- col_factor: float32 [4096], P('mp'), may hold values from 0 to 1, as said below
- step: int32 [1], replicated, may hold values from 2 to 20
Outputs:
- update: float32 [4096, 4096], P('dp', 'mp')
- new_weight: float32 [4096, 4096], P('dp', 'mp')
- row_new: float32 [4096], P('dp')
- col_new: float32 [4096], P('mp')
- next_weight: bfloat16 [4096, 4096], P(None, 'mp')
The draws below stay inside these ranges and needn't reach their ends.
Inputs may be any that keep to these rules, and one draw needn't show every extreme that they name: `row_factor`: positive factors. `col_factor`: positive factors.
All inputs are finite; a program needn't handle non-finite values.
Results may differ from the reference program's by a relative error of at most 0.001.
Values may be sent and summed in bfloat16 or wider, within the bound.
A program may use at most 64 MiB of HBM per device.

```python
import jax
import jax.numpy as jnp
from jax import lax

D = 4096
QW = 4096
TOKENS = 24576


def trend_rows(count):
    return jnp.exp(jnp.log(3.0) * jnp.arange(count, dtype=jnp.float32) / (count - 1))


def draw_master_weight(key, part):
    key = jax.random.fold_in(key, 11)
    first, second = jax.random.split(key)
    row_scale = jnp.exp(jax.random.uniform(first, (D, 1), jnp.float32, jnp.log(0.5), jnp.log(2.0)))
    base = jnp.clip(jax.random.normal(second, (D, QW), jnp.float32), -4.0, 4.0)
    return base * row_scale * trend_rows(D)[:, None]


def draw_row_factor(key, part):
    key = jax.random.fold_in(key, 12)
    level = jnp.exp(jax.random.uniform(key, (D,), jnp.float32, jnp.log(0.05), jnp.log(0.5)))
    return level * trend_rows(D) / TOKENS


def draw_col_factor(key, part):
    key = jax.random.fold_in(key, 13)
    level = jnp.exp(jax.random.uniform(key, (QW,), jnp.float32, jnp.log(0.05), jnp.log(0.5)))
    return level / TOKENS


def raised(values, key, source, target, shards_of, factor):
    def block_of(dim):
        return (jnp.arange(values.shape[dim]) // (values.shape[dim] // shards_of)).reshape((-1,) + (1,) * (values.ndim - 1 - dim))

    near = jax.random.permutation(key, shards_of)[block_of(target)]
    second = (block_of(target) + shards_of // 2) % shards_of
    return jnp.where((block_of(source) == near) | (block_of(source) == second), factor * values, values)


def level_of(stream_key, shape, cuts, smallest, high):
    loudness = 1.0
    for dim, parts in cuts:
        draws = jax.random.uniform(jax.random.fold_in(jax.random.fold_in(stream_key, 6), dim), (parts,), jnp.float32, smallest / len(cuts), high / len(cuts))
        loudness = loudness * jnp.repeat(jnp.exp(draws), shape[dim] // parts).reshape((-1,) + (1,) * (len(shape) - 1 - dim))
    return loudness


def gaussian(stream_key, dims, width, limit, cuts=(), held_as=jnp.bfloat16):
    entries = width * jax.random.normal(stream_key, dims, jnp.float32)
    if cuts:
        entries = entries * level_of(stream_key, dims, cuts, -0.22, 0.18)
    return jnp.clip(entries, -limit, limit).astype(held_as)


def bell_draw_with(own_key, dims, deviation, bound, cuts, heavy, kind=jnp.bfloat16):
    result = deviation * jax.random.normal(own_key, dims, jnp.float32)
    if cuts:
        result = result * level_of(own_key, dims, cuts, -0.22, 0.18)
    return jnp.clip(raised(result, jax.random.fold_in(own_key, 3), *heavy), -bound, bound).astype(kind)


def setup_inputs(seed: int = 0) -> dict:
    streams_of = jax.random.split(jax.random.key(seed), 7)
    inputs = bell_draw_with(streams_of[0], (TOKENS, D), 1.0, 6.0, ((0, 32),), (0, 1, 32, 2.75))
    query_grad = gaussian(streams_of[1], (TOKENS, QW), 1.0, 6.0, ((0, 32), (1, 8)))
    master_weight = draw_master_weight(jax.random.fold_in(streams_of[6], 71), 0)
    row_factor = draw_row_factor(jax.random.fold_in(streams_of[6], 71), 0)
    col_factor = draw_col_factor(jax.random.fold_in(streams_of[6], 71), 0)
    step = jax.random.randint(streams_of[5], (1,), 2, 21).astype(jnp.int32)
    return dict(inputs=inputs, query_grad=query_grad, master_weight=master_weight, row_factor=row_factor, col_factor=col_factor, step=step)


def reference(inputs, query_grad, master_weight, row_factor, col_factor, step):
    summed = lax.dot_general(inputs, query_grad, (((0,), (0,)), ((), ())), preferred_element_type=jnp.float32)
    gradient = summed / TOKENS
    step_value = step[0].astype(jnp.float32)
    decay_rate = 1.0 - step_value ** (-0.8)
    squares = gradient * gradient
    row_new = decay_rate * row_factor + (1.0 - decay_rate) * (lax.optimization_barrier(jnp.mean(squares, 1)) + 1e-30)
    col_new = decay_rate * col_factor + (1.0 - decay_rate) * (lax.optimization_barrier(jnp.mean(squares, 0)) + 1e-30)
    raw_update = gradient * lax.rsqrt(row_new[:, None] * col_new[None, :])
    clip_factor = jnp.maximum(1.0, jnp.sqrt(jnp.mean(raw_update * raw_update)))
    update = raw_update / clip_factor
    weight_norm = jnp.sqrt(jnp.mean(master_weight * master_weight) + 1e-06)
    step_size = 0.01 * weight_norm
    new_weight = master_weight - step_size * update
    next_weight = new_weight.astype(jnp.bfloat16)
    return (update, new_weight, row_new, col_new, next_weight)
```

```python
import functools

import jax
import jax.numpy as jnp
from jax import lax
from jax.experimental import pallas as pl
from jax.experimental.pallas import tpu as pltpu
from jax.sharding import PartitionSpec as P

MESH = pl.DeviceIdType.MESH
NX, NY, NC = 4, 4, 2
NPLANE = NX * NY * NC
FAR = (2, 1, 3, 0)
PEAK = 32766.0
TOP = PEAK * PEAK * (1.0 - 1e-4)


def encode(x, buf):
    h = x.shape[0]
    top = jnp.max(jnp.abs(x), axis=0, keepdims=True)
    e = jnp.ceil(jnp.log2(jnp.maximum(top, 1e-30)))
    t = x * (jnp.exp2(-e) * TOP)
    y = t * lax.rsqrt(jnp.maximum(jnp.abs(t), 1e-12))
    buf[0:h, :] = jnp.round(y).astype(jnp.int32).astype(jnp.int16)
    buf[h : h + 16, :] = jnp.broadcast_to(e.astype(jnp.int32), (16, x.shape[1])).astype(jnp.int16)


def decode(buf, h):
    y = buf[0:h, :].astype(jnp.int32).astype(jnp.float32)
    e = buf[h : h + 16, :].astype(jnp.int32).astype(jnp.float32)[0:1, :]
    return y * jnp.abs(y) * (jnp.exp2(e) * (1.0 / TOP))


def kernel(
    nz, total_tokens, total_rows, total_cols,
    x_hbm, q_hbm, mw_ref, row_ref, col_ref, step_ref,
    upd_ref, nw_ref, rown_ref, coln_ref, out_ref,
    qcat, qT, X, S, R,
    s1a, r1a, s1b, r1b, s2a, r2a, s2b, r2b,
    zr, pr, ta, tb,
    own_sem, qsem, d_send, d_recv,
    s1a_s, s1a_r, s1b_s, s1b_r, s2a_s, s2a_r, s2b_s, s2b_r,
    ex_s, zr_r, pr_r, ta_r, tb_r, zs1, zs2,
    ag_s, a1_r, a2_r, b1_r, b2_r, dd_r, dd2_r,
):
    T, W = q_hbm.shape
    B = W // 1
    H = W // 2
    dp = lax.axis_index("dp")
    z = lax.axis_index("mp")
    c = dp % 2
    cx = dp // (NY * NC)
    cy = (dp // NC) % NY
    sib = dp + 1 - 2 * c
    cs = 1 - c
    u = cx * (1 - c) + cy * c
    w = cy * (1 - c) + cx * c
    su = NY * NC - (NY * NC - NC) * c
    sw = NC + (NY * NC - NC) * c
    us, ws, sus, sws = w, u, sw, su

    def dev(uu, ww):
        return ((uu + 8) % 4) * su + ((ww + 8) % 4) * sw + c

    def sdev(uu, ww):
        return ((uu + 8) % 4) * sus + ((ww + 8) % 4) * sws + cs

    un, up = dev(u + 1, w), dev(u - 1, w)
    wn, wp = dev(u, w + 1), dev(u, w - 1)

    def cols_of(b):
        return pl.ds(pl.multiple_of(b * 128, 128), 128)

    def remote(src, dst, ss, rs, d, zz=None):
        return pltpu.make_async_remote_copy(
            src, dst, ss, rs, device_id=(d, z if zz is None else zz), device_id_type=MESH
        )

    pltpu.make_async_copy(q_hbm, qcat.at[pl.ds(0, T)], qsem).start()
    own = []
    for g in range(4):
        for k in range(4):
            s = 4 * g + k
            cp = pltpu.make_async_copy(
                x_hbm.at[:, cols_of(dev(u + FAR[g], w + FAR[k]))],
                X.at[s // 2, pl.ds(0, T), pl.ds(128 * (s % 2), 128)],
                own_sem.at[s],
            )
            cp.start()
            own.append(cp)

    bar = pltpu.get_barrier_semaphore()
    zn, zp = (z + 1) % nz, (z + nz - 1) % nz
    for d in (sib, un, up, wn, wp):
        pl.semaphore_signal(bar, 1, device_id=(d, z), device_id_type=MESH)
    for zz in (zn, zp):
        pl.semaphore_signal(bar, 1, device_id=(dp, zz), device_id_type=MESH)
    pl.semaphore_wait(bar, 7)

    dq = remote(q_hbm, qcat.at[pl.ds(T, T)], d_send.at[16], d_recv.at[16], sib)
    dq.start()
    dx = []
    for g in range(4):
        for k in range(4):
            s = 4 * g + k
            cp = remote(
                x_hbm.at[:, cols_of(sdev(us + FAR[g], ws + FAR[k]))],
                X.at[s // 2, pl.ds(T, T), pl.ds(128 * (s % 2), 128)],
                d_send.at[s], d_recv.at[s], sib,
            )
            cp.start()
            dx.append(cp)
    for zz in (zn, zp):
        pl.semaphore_signal(zs1, 1, device_id=(dp, zz), device_id_type=MESH)

    pltpu.make_async_copy(q_hbm, qcat.at[pl.ds(0, T)], qsem).wait()
    qT[:, 0:T] = qcat[0:T, :].T
    dq.wait_recv()
    qT[:, T : 2 * T] = qcat[T : 2 * T, :].T

    def matmul(p):
        for s in (2 * p, 2 * p + 1):
            own[s].wait()
            dx[s].wait_recv()
        acc = jnp.dot(qT[...], X[p], preferred_element_type=jnp.float32)
        S[2 * p] = acc[:, 0:128]
        S[2 * p + 1] = acc[:, 128:256]

    c1a = {}
    for p in range(2):
        matmul(p)
        for k in (2 * p, 2 * p + 1):
            for d, to in ((0, un), (1, up)):
                encode(S[k, d * H : d * H + H, :], s1a.at[d, k])
                cp = remote(s1a.at[d, k], r1a.at[d, k], s1a_s.at[d, k], s1a_r.at[d, k], to)
                cp.start()
                c1a[d, k] = cp
    pl.semaphore_wait(zs1, 2)
    for zz in ((z + 2) % nz, (z + nz - 2) % nz):
        pl.semaphore_signal(zs2, 1, device_id=(dp, zz), device_id_type=MESH)
    for p in range(2, 8):
        matmul(p)

    c1b = {}

    def send1b(d, k, h):
        to = un if d == 0 else up
        cp = remote(
            s1b.at[d, k, h], r1b.at[d, k, h], s1b_s.at[d, k, h], s1b_r.at[d, k, h], to
        )
        cp.start()
        c1b[d, k, h] = cp

    for k in range(4):
        for d in range(2):
            g = 1 + d
            h = 1 - d
            encode(S[4 * g + k, h * H : h * H + H, :], s1b.at[d, k, h])
            send1b(d, k, h)
        for d in range(2):
            g = 1 + d
            h = d
            c1a[d, k].wait_recv()
            encode(S[4 * g + k, h * H : h * H + H, :] + decode(r1a.at[d, k], H), s1b.at[d, k, h])
            send1b(d, k, h)

    pl.semaphore_wait(zs2, 2)

    c2a, c2b = {}, {}

    def send2b(d, h):
        to = wn if d == 0 else wp
        cp = remote(s2b.at[d, h], r2b.at[d, h], s2b_s.at[d, h], s2b_r.at[d, h], to)
        cp.start()
        c2b[d, h] = cp

    for k in range(4):
        for h in range(2):
            c1b[0, k, h].wait_recv()
            c1b[1, k, h].wait_recv()
            R[k, h * H : h * H + H, :] = (
                S[12 + k, h * H : h * H + H, :]
                + decode(r1b.at[0, k, h], H)
                + decode(r1b.at[1, k, h], H)
            )
        if k == 0:
            for d, to in ((0, wn), (1, wp)):
                encode(R[0, d * H : d * H + H, :], s2a.at[d])
                cp = remote(s2a.at[d], r2a.at[d], s2a_s.at[d], s2a_r.at[d], to)
                cp.start()
                c2a[d] = cp
        elif k < 3:
            d = k - 1
            h = 1 - d
            encode(R[k, h * H : h * H + H, :], s2b.at[d, h])
            send2b(d, h)
            c2a[d].wait_recv()
            h = d
            encode(R[k, h * H : h * H + H, :] + decode(r2a.at[d], H), s2b.at[d, h])
            send2b(d, h)
    for h in range(2):
        c2b[0, h].wait_recv()
        c2b[1, h].wait_recv()
        R[3, h * H : h * H + H, :] = (
            R[3, h * H : h * H + H, :] + decode(r2b.at[0, h], H) + decode(r2b.at[1, h], H)
        )

    gT = R[3] * (1.0 / total_tokens)
    zr[pl.ds(z, 1)] = jnp.sum(gT * gT, axis=0, keepdims=True)[None]
    gN = gT.T
    pr[pl.ds(dp, 1)] = jnp.sum(gN * gN, axis=0, keepdims=True)[None]

    def to_plane(i, buf, ssem, rsem):
        peer = (dp + i) % NPLANE
        return remote(buf.at[pl.ds(dp, 1)], buf.at[pl.ds(dp, 1)], ssem, rsem, peer)

    def to_z(i, buf, ssem, rsem):
        peer = (z + i) % nz
        return remote(buf.at[pl.ds(z, 1)], buf.at[pl.ds(z, 1)], ssem, rsem, dp, peer)

    def exchange(n, to, buf, ssem, rsem):
        def body(i, carry):
            to(i, buf, ssem, rsem).start()
            return carry

        lax.fori_loop(1, n, body, 0)

    def finish(n, buf, rsem):
        part = buf.at[pl.ds(0, n - 1)]
        cp = pltpu.make_async_copy(part, part, rsem)
        cp.wait()

    exchange(nz, to_z, zr, ex_s.at[0], zr_r)
    exchange(NPLANE, to_plane, pr, ex_s.at[1], pr_r)
    mw = mw_ref[...]
    wsum = jnp.sum(mw * mw)
    stepv = jnp.full((1, 128), step_ref[0].astype(jnp.float32), jnp.float32)
    decay = 1.0 - jnp.exp(-0.8 * jnp.log(stepv))
    decay_w = jnp.concatenate([decay] * (W // 128), axis=1)
    finish(nz, zr, zr_r)
    row_new = decay * row_ref[...] + (1.0 - decay) * (jnp.sum(zr[...], axis=0) / total_cols + 1e-30)
    rown_ref[...] = row_new
    half = (gT * lax.rsqrt(row_new)).T
    finish(NPLANE, pr, pr_r)
    col_new = decay_w * col_ref[...] + (1.0 - decay_w) * (
        jnp.sum(pr[...], axis=0) / total_rows + 1e-30
    )
    coln_ref[...] = col_new
    raw = half * lax.rsqrt(col_new)
    rsum = jnp.sum(raw * raw)

    lane = lax.broadcasted_iota(jnp.int32, (1, 1, 128), 2)
    ta[pl.ds(dp, 1)] = jnp.where(lane < 64, rsum, wsum)
    exchange(NPLANE, to_plane, ta, ex_s.at[2], ta_r)
    finish(NPLANE, ta, ta_r)
    tb[pl.ds(z, 1)] = jnp.sum(ta[...], axis=0, keepdims=True)
    exchange(nz, to_z, tb, ex_s.at[3], tb_r)
    finish(nz, tb, tb_r)
    tot = jnp.sum(tb[...], axis=0) / (total_rows * total_cols)
    clip = jnp.maximum(1.0, jnp.sqrt(tot[:, 0:1]))
    size = 0.01 * jnp.sqrt(tot[:, 64:65] + 1e-06)
    upd = raw * (1.0 / clip)
    nw = mw - size * upd

    def rows_of(b, half=None):
        if half is None:
            return out_ref.at[pl.ds(pl.multiple_of(b * 128, 128), 128)]
        return out_ref.at[pl.ds(pl.multiple_of(b * 128 + half * 64, 64), 64)]

    mine = rows_of(dp)
    mine[...] = nw.astype(jnp.bfloat16)

    sent = []

    def push(b, half, sem, rsem, to):
        cp = remote(rows_of(b, half), rows_of(b, half), sem, rsem, to)
        cp.start()
        sent.append(cp)
        return cp

    n_sent = [0]

    def nsem():
        n_sent[0] += 1
        return ag_s.at[n_sent[0] - 1]

    a1 = {0: push(dp, None, nsem(), a1_r.at[0], wn), 1: push(dp, None, nsem(), a1_r.at[1], wp)}
    b1, b2, dd, dd2, a2 = {}, {}, {}, {}, {}

    def spread(b, k):
        b1[0, k] = push(b, None, nsem(), b1_r.at[0, k], un)
        b1[1, k] = push(b, None, nsem(), b1_r.at[1, k], up)

    def across(b, j):
        dd[j] = push(b, None, nsem(), dd_r.at[j], sib)

    spread(dp, 0)
    across(dp, 0)
    upd_ref[...] = upd
    nw_ref[...] = nw
    a1[0].wait_recv()
    a2[0] = push(wp, 0, nsem(), a2_r.at[0], wn)
    spread(wp, 1)
    a1[1].wait_recv()
    a2[1] = push(wn, 1, nsem(), a2_r.at[1], wp)
    spread(wn, 2)
    across(wp, 1)
    across(wn, 2)

    def onward(k, ww):
        b1[0, k].wait_recv()
        b2[0, k] = push(dev(u - 1, ww), 0, nsem(), b2_r.at[0, k], un)
        across(dev(u - 1, ww), 4 + 2 * k)
        b1[1, k].wait_recv()
        b2[1, k] = push(dev(u + 1, ww), 1, nsem(), b2_r.at[1, k], up)
        across(dev(u + 1, ww), 5 + 2 * k)

    onward(0, w)
    a2[0].wait_recv()
    a2[1].wait_recv()
    wf = dev(u, w + 2)
    spread(wf, 3)
    across(wf, 3)
    onward(1, w - 1)
    onward(2, w + 1)
    onward(3, w + 2)
    for k, ww in ((0, w), (1, w - 1), (2, w + 1), (3, w + 2)):
        b2[0, k].wait_recv()
        b2[1, k].wait_recv()
        dd2[k] = push(dev(u + 2, ww), None, nsem(), dd2_r.at[k], sib)
    for j in range(12):
        dd[j].wait_recv()
    for k in range(4):
        dd2[k].wait_recv()

    for cp in sent:
        cp.wait_send()
    dq.wait_send()
    for cp in dx:
        cp.wait_send()
    for group in (c1a, c1b, c2a, c2b):
        for cp in group.values():
            cp.wait_send()
    for i, (buf, n) in enumerate(((zr, nz), (pr, NPLANE), (ta, NPLANE), (tb, nz))):
        finish(n, buf, ex_s.at[i])


def body(inputs, query_grad, master_weight, row_factor, col_factor, step):
    T, W = query_grad.shape
    rows = inputs.shape[1]
    nz = lax.axis_size("mp")
    ndp = lax.axis_size("dp")
    H = W // 2
    f32, i16, bf16 = jnp.float32, jnp.int16, jnp.bfloat16
    DMA = pltpu.SemaphoreType.DMA
    hb = (H + 16, 128)
    vm = pl.BlockSpec(memory_space=pltpu.VMEM)
    hbm = pl.BlockSpec(memory_space=pl.ANY)
    outs = pl.pallas_call(
        functools.partial(kernel, nz, T * ndp, rows, W * nz),
        out_shape=[
            jax.ShapeDtypeStruct((128, W), f32),
            jax.ShapeDtypeStruct((128, W), f32),
            jax.ShapeDtypeStruct((1, 128), f32),
            jax.ShapeDtypeStruct((1, W), f32),
            pltpu.VMEM((rows, W), bf16),
        ],
        in_specs=[hbm, hbm, vm, vm, vm, pl.BlockSpec(memory_space=pltpu.SMEM)],
        out_specs=[vm, vm, vm, vm, vm],
        scratch_shapes=[
            pltpu.VMEM((2 * T, W), bf16),
            pltpu.VMEM((W, 2 * T), bf16),
            pltpu.VMEM((8, 2 * T, 256), bf16),
            pltpu.VMEM((16, W, 128), f32),
            pltpu.VMEM((4, W, 128), f32),
            pltpu.VMEM((2, 4) + hb, i16),
            pltpu.VMEM((2, 4) + hb, i16),
            pltpu.VMEM((2, 4, 2) + hb, i16),
            pltpu.VMEM((2, 4, 2) + hb, i16),
            pltpu.VMEM((2,) + hb, i16),
            pltpu.VMEM((2,) + hb, i16),
            pltpu.VMEM((2, 2) + hb, i16),
            pltpu.VMEM((2, 2) + hb, i16),
            pltpu.VMEM((nz, 1, 128), f32),
            pltpu.VMEM((NPLANE, 1, W), f32),
            pltpu.VMEM((NPLANE, 1, 128), f32),
            pltpu.VMEM((nz, 1, 128), f32),
            DMA((16,)), DMA, DMA((17,)), DMA((17,)),
            DMA((2, 4)), DMA((2, 4)), DMA((2, 4, 2)), DMA((2, 4, 2)),
            DMA((2,)), DMA((2,)), DMA((2, 2)), DMA((2, 2)),
            DMA((4,)), DMA, DMA, DMA, DMA,
            pltpu.SemaphoreType.REGULAR, pltpu.SemaphoreType.REGULAR,
            DMA((40,)), DMA((2,)), DMA((2,)), DMA((2, 4)), DMA((2, 4)), DMA((12,)), DMA((4,)),
        ],
        compiler_params=pltpu.CompilerParams(
            collective_id=0, has_side_effects=True, vmem_limit_bytes=44 * 2**20
        ),
    )(
        inputs, query_grad, master_weight,
        row_factor.reshape(1, 128), col_factor.reshape(1, W), step,
    )
    return outs[0], outs[1], outs[2].reshape(128), outs[3].reshape(W), outs[4]


def solution(mesh):
    in_specs = (P("dp", None), P("dp", "mp"), P("dp", "mp"), P("dp"), P("mp"), P())
    out_specs = (P("dp", "mp"), P("dp", "mp"), P("dp"), P("mp"), P(None, "mp"))
    return jax.shard_map(body, mesh=mesh, in_specs=in_specs, out_specs=out_specs, check_vma=False)
```

```python
import functools

import jax
import jax.numpy as jnp
from jax import lax
from jax.experimental import pallas as pl
from jax.experimental.pallas import tpu as pltpu
from jax.sharding import PartitionSpec as P

MESH = pl.DeviceIdType.MESH
NX, NY, NC = 4, 4, 2
NPLANE = NX * NY * NC
FAR = (2, 1, 3, 0)
PEAK = 32766.0
TOP = PEAK * PEAK * (1.0 - 1e-4)


def encode(x, buf):
    h = x.shape[0]
    top = jnp.max(jnp.abs(x), axis=0, keepdims=True)
    e = jnp.ceil(jnp.log2(jnp.maximum(top, 1e-30)))
    t = x * (jnp.exp2(-e) * TOP)
    y = t * lax.rsqrt(jnp.maximum(jnp.abs(t), 1e-12))
    buf[0:h, :] = jnp.round(y).astype(jnp.int32).astype(jnp.int16)
    buf[h : h + 16, :] = jnp.broadcast_to(e.astype(jnp.int32), (16, x.shape[1])).astype(jnp.int16)


def decode(buf, h):
    y = buf[0:h, :].astype(jnp.int32).astype(jnp.float32)
    e = buf[h : h + 16, :].astype(jnp.int32).astype(jnp.float32)[0:1, :]
    return y * jnp.abs(y) * (jnp.exp2(e) * (1.0 / TOP))


def kernel(
    nz, total_tokens, total_rows, total_cols,
    x_hbm, q_hbm, mw_hbm, row_hbm, col_hbm, step_ref,
    upd_ref, nw_ref, rown_ref, coln_ref, out_ref,
    mw_ref, row_ref, col_ref, p_sem,
    qcat, qT, X, S, R, sd, rd,
    s1a, r1a, s1b, r1b, s2a, r2a, s2b, r2b,
    zr, pr, ta, tb,
    own_sem, qsem, d_send, d_recv,
    s1a_s, s1a_r, s1b_s, s1b_r, s2a_s, s2a_r, s2b_s, s2b_r,
    ex_s, zr_r, pr_r, ta_r, tb_r, zs1, zs2,
    ag_s, a1_r, a2_r, b1_r, b2_r, dd_r,
):
    T, W = q_hbm.shape
    H = W // 2
    dp = lax.axis_index("dp")
    z = lax.axis_index("mp")
    c = dp % 2
    cx = dp // (NY * NC)
    cy = (dp // NC) % NY
    sib = dp + 1 - 2 * c
    cs = 1 - c
    u = cx * (1 - c) + cy * c
    w = cy * (1 - c) + cx * c
    su = NY * NC - (NY * NC - NC) * c
    sw = NC + (NY * NC - NC) * c
    us, ws, sus, sws = w, u, sw, su

    def dev(uu, ww):
        return ((uu + 8) % 4) * su + ((ww + 8) % 4) * sw + c

    def sdev(uu, ww):
        return ((uu + 8) % 4) * sus + ((ww + 8) % 4) * sws + cs

    un, up = dev(u + 1, w), dev(u - 1, w)
    wn, wp = dev(u, w + 1), dev(u, w - 1)

    def cols_of(b):
        return pl.ds(pl.multiple_of(b * 128, 128), 128)

    def remote(src, dst, ss, rs, d, zz=None):
        return pltpu.make_async_remote_copy(
            src, dst, ss, rs, device_id=(d, z if zz is None else zz), device_id_type=MESH
        )

    cq = pltpu.make_async_copy(q_hbm, qcat, qsem)
    cq.start()
    loads = {}

    def load(side, p):
        for s in (2 * p, 2 * p + 1):
            o = (FAR[s // 4], FAR[s % 4])
            b = dev(u + o[0], w + o[1]) if side else sdev(us + o[0], ws + o[1])
            j = 16 * side + s
            cp = pltpu.make_async_copy(
                x_hbm.at[:, cols_of(b)],
                X.at[j // 2, :, pl.ds(128 * (j % 2), 128)],
                own_sem.at[j],
            )
            cp.start()
            loads[j] = cp

    for side, p in ((0, 0), (0, 1)):
        load(side, p)

    bar = pltpu.get_barrier_semaphore()
    zn, zp = (z + 1) % nz, (z + nz - 1) % nz
    for d in (sib, un, up, wn, wp):
        pl.semaphore_signal(bar, 1, device_id=(d, z), device_id_type=MESH)
    for zz in (zn, zp):
        pl.semaphore_signal(bar, 1, device_id=(dp, zz), device_id_type=MESH)

    for side, p in (
        (1, 0), (1, 1), (0, 2), (0, 4), (0, 3), (0, 5),
        (1, 2), (1, 4), (1, 3), (1, 5), (0, 6), (0, 7), (1, 6), (1, 7),
    ):
        load(side, p)
    cq.wait()
    qT[...] = qcat[...].T

    def matmul(side, p):
        j = 8 * side + p
        loads[2 * j].wait()
        loads[2 * j + 1].wait()
        return jnp.dot(qT[...], X[j], preferred_element_type=jnp.float32)

    def theirs(p):
        acc = matmul(0, p)
        for i in range(2):
            for h in range(2):
                encode(acc[h * H : h * H + H, 128 * i : 128 * i + 128], sd.at[2 * p + i, h])

    cd = {}

    def give(p):
        for s in (2 * p, 2 * p + 1):
            cd[s] = remote(sd.at[s], rd.at[s], d_send.at[s], d_recv.at[s], sib)
            cd[s].start()

    def mine(p):
        acc = matmul(1, p)
        S[2 * p] = acc[:, 0:128]
        S[2 * p + 1] = acc[:, 128:256]

    def total(s):
        cd[s].wait_recv()
        for h in range(2):
            S[s, h * H : h * H + H, :] = S[s, h * H : h * H + H, :] + decode(rd.at[s, h], H)

    theirs(0)
    pl.semaphore_wait(bar, 7)
    give(0)
    theirs(1)
    give(1)
    params = [
        pltpu.make_async_copy(a, b, p_sem.at[i])
        for i, (a, b) in enumerate(((mw_hbm, mw_ref), (row_hbm, row_ref), (col_hbm, col_ref)))
    ]
    for cp in params:
        cp.start()

    for zz in (zn, zp):
        pl.semaphore_signal(zs1, 1, device_id=(dp, zz), device_id_type=MESH)
    mine(0)
    mine(1)
    theirs(2)
    give(2)

    c1a = {}
    for k in range(4):
        total(k)
        for d in range(2):
            encode(S[k, d * H : d * H + H, :], s1a.at[d, k])
        for d, to in ((0, un), (1, up)):
            cp = remote(s1a.at[d, k], r1a.at[d, k], s1a_s.at[d, k], s1a_r.at[d, k], to)
            cp.start()
            c1a[d, k] = cp
    pl.semaphore_wait(zs1, 2)
    for zz in ((z + 2) % nz, (z + nz - 2) % nz):
        pl.semaphore_signal(zs2, 1, device_id=(dp, zz), device_id_type=MESH)

    c1b = {}

    def send1b(d, k, h):
        to = un if d == 0 else up
        cp = remote(
            s1b.at[d, k, h], r1b.at[d, k, h], s1b_s.at[d, k, h], s1b_r.at[d, k, h], to
        )
        cp.start()
        c1b[d, k, h] = cp

    def at_once(k):
        for d in range(2):
            h = 1 - d
            total(4 * (1 + d) + k)
            encode(S[4 * (1 + d) + k, h * H : h * H + H, :], s1b.at[d, k, h])
        for d in range(2):
            send1b(d, k, 1 - d)

    def with_far(k):
        for d in range(2):
            h = d
            c1a[d, k].wait_recv()
            encode(
                S[4 * (1 + d) + k, h * H : h * H + H, :] + decode(r1a.at[d, k], H),
                s1b.at[d, k, h],
            )
        for d in range(2):
            send1b(d, k, d)

    theirs(4)
    give(4)
    mine(2)
    mine(4)
    at_once(0)
    at_once(1)
    for p in (3, 5):
        theirs(p)
        give(p)
    mine(3)
    mine(5)
    with_far(0)
    at_once(2)
    with_far(1)
    theirs(6)
    give(6)
    at_once(3)
    with_far(2)
    theirs(7)
    give(7)
    mine(6)
    with_far(3)
    mine(7)
    for s in range(12, 16):
        total(s)

    pl.semaphore_wait(zs2, 2)

    c2a, c2b = {}, {}

    def send2b(d, h):
        to = wn if d == 0 else wp
        cp = remote(s2b.at[d, h], r2b.at[d, h], s2b_s.at[d, h], s2b_r.at[d, h], to)
        cp.start()
        c2b[d, h] = cp

    for k in range(4):
        for h in range(2):
            c1b[0, k, h].wait_recv()
            c1b[1, k, h].wait_recv()
            R[k, h * H : h * H + H, :] = (
                S[12 + k, h * H : h * H + H, :]
                + decode(r1b.at[0, k, h], H)
                + decode(r1b.at[1, k, h], H)
            )
        if k == 0:
            for d, to in ((0, wn), (1, wp)):
                encode(R[0, d * H : d * H + H, :], s2a.at[d])
                cp = remote(s2a.at[d], r2a.at[d], s2a_s.at[d], s2a_r.at[d], to)
                cp.start()
                c2a[d] = cp
        elif k < 3:
            d = k - 1
            h = 1 - d
            encode(R[k, h * H : h * H + H, :], s2b.at[d, h])
            send2b(d, h)
            c2a[d].wait_recv()
            h = d
            encode(R[k, h * H : h * H + H, :] + decode(r2a.at[d], H), s2b.at[d, h])
            send2b(d, h)
    for h in range(2):
        c2b[0, h].wait_recv()
        c2b[1, h].wait_recv()
        R[3, h * H : h * H + H, :] = (
            R[3, h * H : h * H + H, :] + decode(r2b.at[0, h], H) + decode(r2b.at[1, h], H)
        )

    for cp in params:
        cp.wait()
    gT = R[3] * (1.0 / total_tokens)
    zr[pl.ds(z, 1)] = jnp.sum(gT * gT, axis=0, keepdims=True)[None]
    gN = gT.T
    pr[pl.ds(dp, 1)] = jnp.sum(gN * gN, axis=0, keepdims=True)[None]

    def to_plane(i, buf, ssem, rsem):
        peer = (dp + i) % NPLANE
        return remote(buf.at[pl.ds(dp, 1)], buf.at[pl.ds(dp, 1)], ssem, rsem, peer)

    def to_z(i, buf, ssem, rsem):
        peer = (z + i) % nz
        return remote(buf.at[pl.ds(z, 1)], buf.at[pl.ds(z, 1)], ssem, rsem, dp, peer)

    def exchange(n, to, buf, ssem, rsem):
        def body(i, carry):
            to(i, buf, ssem, rsem).start()
            return carry

        lax.fori_loop(1, n, body, 0)

    def finish(n, buf, rsem):
        part = buf.at[pl.ds(0, n - 1)]
        cp = pltpu.make_async_copy(part, part, rsem)
        cp.wait()

    exchange(nz, to_z, zr, ex_s.at[0], zr_r)
    exchange(NPLANE, to_plane, pr, ex_s.at[1], pr_r)
    mw = mw_ref[...]
    wsum = jnp.sum(mw * mw)
    stepv = jnp.full((1, 128), step_ref[0].astype(jnp.float32), jnp.float32)
    decay = 1.0 - jnp.exp(-0.8 * jnp.log(stepv))
    decay_w = jnp.concatenate([decay] * (W // 128), axis=1)
    finish(nz, zr, zr_r)
    row_new = decay * row_ref[...] + (1.0 - decay) * (jnp.sum(zr[...], axis=0) / total_cols + 1e-30)
    rown_ref[...] = row_new
    half = (gT * lax.rsqrt(row_new)).T
    finish(NPLANE, pr, pr_r)
    col_new = decay_w * col_ref[...] + (1.0 - decay_w) * (
        jnp.sum(pr[...], axis=0) / total_rows + 1e-30
    )
    coln_ref[...] = col_new
    raw = half * lax.rsqrt(col_new)
    rsum = jnp.sum(raw * raw)

    lane = lax.broadcasted_iota(jnp.int32, (1, 1, 128), 2)
    ta[pl.ds(dp, 1)] = jnp.where(lane < 64, rsum, wsum)
    exchange(NPLANE, to_plane, ta, ex_s.at[2], ta_r)
    finish(NPLANE, ta, ta_r)
    tb[pl.ds(z, 1)] = jnp.sum(ta[...], axis=0, keepdims=True)
    exchange(nz, to_z, tb, ex_s.at[3], tb_r)
    finish(nz, tb, tb_r)
    tot = jnp.sum(tb[...], axis=0) / (total_rows * total_cols)
    clip = jnp.maximum(1.0, jnp.sqrt(tot[:, 0:1]))
    size = 0.01 * jnp.sqrt(tot[:, 64:65] + 1e-06)
    upd = raw * (1.0 / clip)
    nw = mw - size * upd

    def rows_of(b, half=None):
        if half is None:
            return out_ref.at[pl.ds(pl.multiple_of(b * 128, 128), 128)]
        return out_ref.at[pl.ds(pl.multiple_of(b * 128 + half * 64, 64), 64)]

    rows_of(dp)[...] = nw.astype(jnp.bfloat16)

    sent = []

    def push(b, half, rsem, to):
        cp = remote(rows_of(b, half), rows_of(b, half), ag_s.at[len(sent)], rsem, to)
        cp.start()
        sent.append(cp)
        return cp

    a1, a2, b1, b2, dd = {}, {}, {}, {}, {}
    for i in range(2):
        a1[0, i] = push(dp, i, a1_r.at[0, i], wn)
        a1[1, 1 - i] = push(dp, 1 - i, a1_r.at[1, 1 - i], wp)

    def spread(b, k, h):
        b1[0, k, h] = push(b, h, b1_r.at[0, k, h], un)
        b1[1, k, h] = push(b, h, b1_r.at[1, k, h], up)

    def across(b, j, h):
        dd[j, h] = push(b, h, dd_r.at[j, h], sib)

    def both(b, k):
        b1[0, k, 0] = push(b, 0, b1_r.at[0, k, 0], un)
        b1[1, k, 1] = push(b, 1, b1_r.at[1, k, 1], up)
        b1[0, k, 1] = push(b, 1, b1_r.at[0, k, 1], un)
        b1[1, k, 0] = push(b, 0, b1_r.at[1, k, 0], up)
        for h in range(2):
            across(b, k, h)

    both(dp, 0)
    upd_ref[...] = upd
    nw_ref[...] = nw
    a1[0, 0].wait_recv()
    a2[0] = push(wp, 0, a2_r.at[0], wn)
    a1[1, 1].wait_recv()
    a2[1] = push(wn, 1, a2_r.at[1], wp)
    a1[0, 1].wait_recv()
    both(wp, 1)
    a1[1, 0].wait_recv()
    both(wn, 2)

    def onward(k, ww):
        left, right = dev(u - 1, ww), dev(u + 1, ww)
        b1[0, k, 0].wait_recv()
        b2[0, k] = push(left, 0, b2_r.at[0, k], un)
        b1[1, k, 1].wait_recv()
        b2[1, k] = push(right, 1, b2_r.at[1, k], up)
        across(left, 4 + 2 * k, 0)
        across(right, 5 + 2 * k, 1)
        b1[0, k, 1].wait_recv()
        across(left, 4 + 2 * k, 1)
        b1[1, k, 0].wait_recv()
        across(right, 5 + 2 * k, 0)

    onward(0, w)
    wf = dev(u, w + 2)
    for h in range(2):
        a2[h].wait_recv()
        spread(wf, 3, h)
        across(wf, 3, h)
    onward(1, w - 1)
    onward(2, w + 1)
    onward(3, w + 2)
    for k, ww in ((0, w), (1, w - 1), (2, w + 1), (3, w + 2)):
        for h in range(2):
            b2[h, k].wait_recv()
            across(dev(u + 2, ww), 12 + k, h)
    for cp in dd.values():
        cp.wait_recv()

    for cp in sent:
        cp.wait_send()
    for group in (cd, c1a, c1b, c2a, c2b):
        for cp in group.values():
            cp.wait_send()
    for i, (buf, n) in enumerate(((zr, nz), (pr, NPLANE), (ta, NPLANE), (tb, nz))):
        finish(n, buf, ex_s.at[i])


def store(a, b, c, d, e, ao, bo, co, do, eo, sem):
    rows = e.shape[0] // 8
    pairs = [(e.at[pl.ds(i * rows, rows)], eo.at[pl.ds(i * rows, rows)]) for i in range(8)]
    pairs += [(a, ao), (b, bo), (c, co), (d, do)]
    copies = [pltpu.make_async_copy(i, o, sem.at[n]) for n, (i, o) in enumerate(pairs)]
    for cp in copies:
        cp.start()
    for cp in copies:
        cp.wait()


def body(inputs, query_grad, master_weight, row_factor, col_factor, step):
    T, W = query_grad.shape
    rows = inputs.shape[1]
    nz = lax.axis_size("mp")
    ndp = lax.axis_size("dp")
    H = W // 2
    f32, i16, bf16 = jnp.float32, jnp.int16, jnp.bfloat16
    DMA = pltpu.SemaphoreType.DMA
    hb = (H + 16, 128)
    vm = pl.BlockSpec(memory_space=pltpu.VMEM)
    hbm = pl.BlockSpec(memory_space=pltpu.HBM)
    outs = pl.pallas_call(
        functools.partial(kernel, nz, T * ndp, rows, W * nz),
        out_shape=[
            pltpu.VMEM((128, W), f32),
            pltpu.VMEM((128, W), f32),
            pltpu.VMEM((1, 128), f32),
            pltpu.VMEM((1, W), f32),
            pltpu.VMEM((rows, W), bf16),
        ],
        in_specs=[hbm] * 5 + [pl.BlockSpec(memory_space=pltpu.SMEM)],
        out_specs=[vm, vm, vm, vm, vm],
        scratch_shapes=[
            pltpu.VMEM((128, W), f32),
            pltpu.VMEM((1, 128), f32),
            pltpu.VMEM((1, W), f32),
            DMA((3,)),
            pltpu.VMEM((T, W), bf16),
            pltpu.VMEM((W, T), bf16),
            pltpu.VMEM((16, T, 256), bf16),
            pltpu.VMEM((16, W, 128), f32),
            pltpu.VMEM((4, W, 128), f32),
            pltpu.VMEM((16, 2) + hb, i16),
            pltpu.VMEM((16, 2) + hb, i16),
            pltpu.VMEM((2, 4) + hb, i16),
            pltpu.VMEM((2, 4) + hb, i16),
            pltpu.VMEM((2, 4, 2) + hb, i16),
            pltpu.VMEM((2, 4, 2) + hb, i16),
            pltpu.VMEM((2,) + hb, i16),
            pltpu.VMEM((2,) + hb, i16),
            pltpu.VMEM((2, 2) + hb, i16),
            pltpu.VMEM((2, 2) + hb, i16),
            pltpu.VMEM((nz, 1, 128), f32),
            pltpu.VMEM((NPLANE, 1, W), f32),
            pltpu.VMEM((NPLANE, 1, 128), f32),
            pltpu.VMEM((nz, 1, 128), f32),
            DMA((32,)), DMA, DMA((16,)), DMA((16,)),
            DMA((2, 4)), DMA((2, 4)), DMA((2, 4, 2)), DMA((2, 4, 2)),
            DMA((2,)), DMA((2,)), DMA((2, 2)), DMA((2, 2)),
            DMA((4,)), DMA, DMA, DMA, DMA,
            pltpu.SemaphoreType.REGULAR, pltpu.SemaphoreType.REGULAR,
            DMA((64,)), DMA((2, 2)), DMA((2,)), DMA((2, 4, 2)), DMA((2, 4)), DMA((16, 2)),
        ],
        compiler_params=pltpu.CompilerParams(
            collective_id=0, has_side_effects=True, vmem_limit_bytes=44 * 2**20
        ),
    )(*[
        pltpu.with_memory_space_constraint(a, pltpu.HBM)
        for a in (
            inputs, query_grad, master_weight,
            row_factor.reshape(1, 128), col_factor.reshape(1, W),
        )
    ], step)
    outs = pl.pallas_call(
        store,
        out_shape=[jax.ShapeDtypeStruct(o.shape, o.dtype) for o in outs],
        in_specs=[vm] * 5,
        out_specs=[hbm] * 5,
        scratch_shapes=[DMA((12,))],
        compiler_params=pltpu.CompilerParams(vmem_limit_bytes=8 * 2**20),
    )(*outs)
    return outs[0], outs[1], outs[2].reshape(128), outs[3].reshape(W), outs[4]


def solution(mesh):
    in_specs = (P("dp", None), P("dp", "mp"), P("dp", "mp"), P("dp"), P("mp"), P())
    out_specs = (P("dp", "mp"), P("dp", "mp"), P("dp"), P("mp"), P(None, "mp"))
    return jax.shard_map(body, mesh=mesh, in_specs=in_specs, out_specs=out_specs, check_vma=False)
```

```python
import functools

import jax
import jax.numpy as jnp
from jax import lax
from jax.experimental import pallas as pl
from jax.experimental.pallas import tpu as pltpu
from jax.sharding import PartitionSpec as P

MESH = pl.DeviceIdType.MESH
NX, NY, NC = 4, 4, 2
NPLANE = NX * NY * NC
FAR = (2, 1, 3, 0)
PEAK = 32766.0
TOP = PEAK * PEAK * (1.0 - 1e-4)


def encode(x, buf):
    h = x.shape[0]
    top = jnp.max(jnp.abs(x), axis=0, keepdims=True)
    e = jnp.ceil(jnp.log2(jnp.maximum(top, 1e-30)))
    t = x * (jnp.exp2(-e) * TOP)
    y = t * lax.rsqrt(jnp.maximum(jnp.abs(t), 1e-12))
    buf[0:h, :] = jnp.round(y).astype(jnp.int32).astype(jnp.int16)
    buf[h : h + 16, :] = jnp.broadcast_to(e.astype(jnp.int32), (16, x.shape[1])).astype(jnp.int16)


def decode(buf, h):
    y = buf[0:h, :].astype(jnp.int32).astype(jnp.float32)
    e = buf[h : h + 16, :].astype(jnp.int32).astype(jnp.float32)[0:1, :]
    return y * jnp.abs(y) * (jnp.exp2(e) * (1.0 / TOP))


def kernel(
    nz, total_tokens, total_rows, total_cols,
    x_hbm, q_hbm, mw_hbm, row_hbm, col_hbm, step_ref,
    upd_ref, nw_ref, rown_ref, coln_ref, out_ref,
    mw_ref, row_ref, col_ref, p_sem,
    qcat, qT, X, S, R, sd, rd,
    s1a, r1a, s1b, r1b, s2a, r2a, s2b, r2b,
    zr, pr, ta, tb,
    own_sem, qsem, d_send, d_recv,
    s1a_s, s1a_r, s1b_s, s1b_r, s2a_s, s2a_r, s2b_s, s2b_r,
    ex_s, zr_r, pr_r, ta_r, tb_r, zs1, zs2,
    ag_s, a1_r, a2_r, b1_r, b2_r, dd_r,
):
    T, W = q_hbm.shape
    H = W // 2
    dp = lax.axis_index("dp")
    z = lax.axis_index("mp")
    c = lax.rem(dp, NC)
    cx = lax.div(dp, NY * NC)
    cy = lax.rem(lax.div(dp, NC), NY)
    sib = dp + 1 - 2 * c
    cs = 1 - c
    u = cx * (1 - c) + cy * c
    w = cy * (1 - c) + cx * c
    su = NY * NC - (NY * NC - NC) * c
    sw = NC + (NY * NC - NC) * c
    ru = [lax.rem(u + i, 4) * su for i in range(4)]
    rw = [lax.rem(w + i, 4) * sw for i in range(4)]
    rx = [lax.rem(cx + i, NX) * (NY * NC) for i in range(NX)]
    ry = [lax.rem(cy + i, NY) * NC for i in range(NY)]
    rz = [lax.rem(z + i, nz) for i in range(nz)]

    def dev(i, j):
        return ru[i % 4] + rw[j % 4] + c

    def sdev(i, j):
        return rw[i % 4] + ru[j % 4] + cs

    un, up = dev(1, 0), dev(-1, 0)
    wn, wp = dev(0, 1), dev(0, -1)

    def cols_of(b):
        return pl.ds(pl.multiple_of(b * 128, 128), 128)

    def remote(src, dst, ss, rs, d, zz=None):
        return pltpu.make_async_remote_copy(
            src, dst, ss, rs, device_id=(d, z if zz is None else zz), device_id_type=MESH
        )

    cq = pltpu.make_async_copy(q_hbm, qcat, qsem)
    cq.start()
    loads = {}

    def load(side, p):
        for s in (2 * p, 2 * p + 1):
            o = (FAR[s // 4], FAR[s % 4])
            b = dev(*o) if side else sdev(*o)
            j = 16 * side + s
            cp = pltpu.make_async_copy(
                x_hbm.at[:, cols_of(b)],
                X.at[j // 2, :, pl.ds(128 * (j % 2), 128)],
                own_sem.at[j],
            )
            cp.start()
            loads[j] = cp

    for side, p in ((0, 0), (0, 1)):
        load(side, p)

    bar = pltpu.get_barrier_semaphore()
    zn, zp = rz[1 % nz], rz[nz - 1]
    for d in (sib, un, up, wn, wp):
        pl.semaphore_signal(bar, 1, device_id=(d, z), device_id_type=MESH)
    for zz in (zn, zp):
        pl.semaphore_signal(bar, 1, device_id=(dp, zz), device_id_type=MESH)

    for side, p in (
        (1, 0), (1, 1), (0, 2), (0, 4), (0, 3), (0, 5),
        (1, 2), (1, 4), (1, 3), (1, 5), (0, 6), (0, 7), (1, 6), (1, 7),
    ):
        load(side, p)
    cq.wait()
    qT[...] = qcat[...].T

    def matmul(side, p):
        j = 8 * side + p
        loads[2 * j].wait()
        loads[2 * j + 1].wait()
        return jnp.dot(qT[...], X[j], preferred_element_type=jnp.float32)

    def theirs(p):
        acc = matmul(0, p)
        for i in range(2):
            for h in range(2):
                encode(acc[h * H : h * H + H, 128 * i : 128 * i + 128], sd.at[2 * p + i, h])

    cd = {}

    def give(p):
        for s in (2 * p, 2 * p + 1):
            cd[s] = remote(sd.at[s], rd.at[s], d_send.at[s], d_recv.at[s], sib)
            cd[s].start()

    def mine(p):
        acc = matmul(1, p)
        S[2 * p] = acc[:, 0:128]
        S[2 * p + 1] = acc[:, 128:256]

    def total(s):
        cd[s].wait_recv()
        for h in range(2):
            S[s, h * H : h * H + H, :] = S[s, h * H : h * H + H, :] + decode(rd.at[s, h], H)

    theirs(0)
    pl.semaphore_wait(bar, 7)
    give(0)
    theirs(1)
    give(1)
    params = [
        pltpu.make_async_copy(a, b, p_sem.at[i])
        for i, (a, b) in enumerate(((mw_hbm, mw_ref), (row_hbm, row_ref), (col_hbm, col_ref)))
    ]
    for cp in params:
        cp.start()

    for zz in (zn, zp):
        pl.semaphore_signal(zs1, 1, device_id=(dp, zz), device_id_type=MESH)
    mine(0)
    mine(1)
    theirs(2)
    give(2)

    c1a = {}
    for k in range(4):
        total(k)
        for d in range(2):
            encode(S[k, d * H : d * H + H, :], s1a.at[d, k])
        for d, to in ((0, un), (1, up)):
            cp = remote(s1a.at[d, k], r1a.at[d, k], s1a_s.at[d, k], s1a_r.at[d, k], to)
            cp.start()
            c1a[d, k] = cp
    pl.semaphore_wait(zs1, 2)
    for zz in (rz[2 % nz], rz[nz - 2]):
        pl.semaphore_signal(zs2, 1, device_id=(dp, zz), device_id_type=MESH)

    c1b = {}

    def send1b(d, k, h):
        to = un if d == 0 else up
        cp = remote(
            s1b.at[d, k, h], r1b.at[d, k, h], s1b_s.at[d, k, h], s1b_r.at[d, k, h], to
        )
        cp.start()
        c1b[d, k, h] = cp

    def at_once(k):
        for d in range(2):
            h = 1 - d
            total(4 * (1 + d) + k)
            encode(S[4 * (1 + d) + k, h * H : h * H + H, :], s1b.at[d, k, h])
        for d in range(2):
            send1b(d, k, 1 - d)

    def with_far(k):
        for d in range(2):
            h = d
            c1a[d, k].wait_recv()
            encode(
                S[4 * (1 + d) + k, h * H : h * H + H, :] + decode(r1a.at[d, k], H),
                s1b.at[d, k, h],
            )
        for d in range(2):
            send1b(d, k, d)

    c2a, c2b = {}, {}

    def send2b(d, h):
        to = wn if d == 0 else wp
        cp = remote(s2b.at[d, h], r2b.at[d, h], s2b_s.at[d, h], s2b_r.at[d, h], to)
        cp.start()
        c2b[d, h] = cp

    def gathered(k, h):
        c1b[0, k, h].wait_recv()
        c1b[1, k, h].wait_recv()
        R[k, h * H : h * H + H, :] = (
            S[12 + k, h * H : h * H + H, :]
            + decode(r1b.at[0, k, h], H)
            + decode(r1b.at[1, k, h], H)
        )

    def second(k):
        if k == 0:
            gathered(k, 0)
            gathered(k, 1)
            for d, to in ((0, wn), (1, wp)):
                encode(R[0, d * H : d * H + H, :], s2a.at[d])
                cp = remote(s2a.at[d], r2a.at[d], s2a_s.at[d], s2a_r.at[d], to)
                cp.start()
                c2a[d] = cp
        else:
            d = k - 1
            gathered(k, 1 - d)
            encode(R[k, (1 - d) * H : (1 - d) * H + H, :], s2b.at[d, 1 - d])
            send2b(d, 1 - d)
            gathered(k, d)

    def second_far(k):
        d = k - 1
        c2a[d].wait_recv()
        encode(R[k, d * H : d * H + H, :] + decode(r2a.at[d], H), s2b.at[d, d])
        send2b(d, d)

    theirs(4)
    give(4)
    mine(2)
    mine(4)
    at_once(0)
    at_once(1)
    for p in (3, 5):
        theirs(p)
        give(p)
    mine(3)
    mine(5)
    with_far(0)
    at_once(2)
    at_once(3)
    with_far(1)
    for p in (6, 7):
        theirs(p)
        give(p)
    with_far(2)
    mine(6)
    mine(7)
    with_far(3)
    for s in range(12, 16):
        total(s)
    pl.semaphore_wait(zs2, 2)
    second(0)
    second(1)
    second(2)
    second_far(1)
    second_far(2)
    gathered(3, 0)
    gathered(3, 1)
    for h in range(2):
        c2b[0, h].wait_recv()
        c2b[1, h].wait_recv()
        R[3, h * H : h * H + H, :] = (
            R[3, h * H : h * H + H, :] + decode(r2b.at[0, h], H) + decode(r2b.at[1, h], H)
        )

    for cp in params:
        cp.wait()
    gT = R[3] * (1.0 / total_tokens)
    zr[pl.ds(z, 1)] = jnp.sum(gT * gT, axis=0, keepdims=True)[None]
    gN = gT.T
    pr[pl.ds(dp, 1)] = jnp.sum(gN * gN, axis=0, keepdims=True)[None]

    far_plane = sorted(
        ((i, j, k) for i in range(NX) for j in range(NY) for k in range(NC) if i or j or k),
        key=lambda o: -(min(o[0], NX - o[0]) + min(o[1], NY - o[1])),
    )
    far_z = sorted(range(1, nz), key=lambda i: -min(i, nz - i))

    def to_plane(buf, ssem, rsem):
        for i, j, k in far_plane:
            peer = rx[i] + ry[j] + (cs if k else c)
            remote(buf.at[pl.ds(dp, 1)], buf.at[pl.ds(dp, 1)], ssem, rsem, peer).start()

    def to_z(buf, ssem, rsem):
        for i in far_z:
            remote(buf.at[pl.ds(z, 1)], buf.at[pl.ds(z, 1)], ssem, rsem, dp, rz[i]).start()

    def finish(n, buf, rsem):
        part = buf.at[pl.ds(0, n - 1)]
        cp = pltpu.make_async_copy(part, part, rsem)
        cp.wait()

    to_z(zr, ex_s.at[0], zr_r)
    to_plane(pr, ex_s.at[1], pr_r)
    mw = mw_ref[...]
    wsum = jnp.sum(mw * mw)
    stepv = jnp.full((1, 128), step_ref[0].astype(jnp.float32), jnp.float32)
    decay = 1.0 - jnp.exp(-0.8 * jnp.log(stepv))
    decay_w = jnp.concatenate([decay] * (W // 128), axis=1)
    finish(nz, zr, zr_r)
    row_new = decay * row_ref[...] + (1.0 - decay) * (jnp.sum(zr[...], axis=0) / total_cols + 1e-30)
    rown_ref[...] = row_new
    half = (gT * lax.rsqrt(row_new)).T
    finish(NPLANE, pr, pr_r)
    col_new = decay_w * col_ref[...] + (1.0 - decay_w) * (
        jnp.sum(pr[...], axis=0) / total_rows + 1e-30
    )
    coln_ref[...] = col_new
    raw = half * lax.rsqrt(col_new)
    rsum = jnp.sum(raw * raw)

    lane = lax.broadcasted_iota(jnp.int32, (1, 1, 128), 2)
    ta[pl.ds(dp, 1)] = jnp.where(lane < 64, rsum, wsum)
    to_plane(ta, ex_s.at[2], ta_r)
    for group in (cd, c1a, c1b, c2a, c2b):
        for cp in group.values():
            cp.wait_send()
    finish(NPLANE, ta, ta_r)
    tb[pl.ds(z, 1)] = jnp.sum(ta[...], axis=0, keepdims=True)
    to_z(tb, ex_s.at[3], tb_r)
    finish(nz, tb, tb_r)
    tot = jnp.sum(tb[...], axis=0) / (total_rows * total_cols)
    clip = jnp.maximum(1.0, jnp.sqrt(tot[:, 0:1]))
    size = 0.01 * jnp.sqrt(tot[:, 64:65] + 1e-06)
    upd = raw * (1.0 / clip)
    nw = mw - size * upd

    def rows_of(b, half=None):
        if half is None:
            return out_ref.at[pl.ds(pl.multiple_of(b * 128, 128), 128)]
        return out_ref.at[pl.ds(pl.multiple_of(b * 128 + half * 64, 64), 64)]

    rows_of(dp)[...] = nw.astype(jnp.bfloat16)

    sent = []

    def push(b, half, rsem, to):
        cp = remote(rows_of(b, half), rows_of(b, half), ag_s.at[len(sent)], rsem, to)
        cp.start()
        sent.append(cp)
        return cp

    a1, a2, b1, b2, dd = {}, {}, {}, {}, {}
    for i in range(2):
        a1[0, i] = push(dp, i, a1_r.at[0, i], wn)
        a1[1, 1 - i] = push(dp, 1 - i, a1_r.at[1, 1 - i], wp)

    def spread(b, k, h):
        b1[0, k, h] = push(b, h, b1_r.at[0, k, h], un)
        b1[1, k, h] = push(b, h, b1_r.at[1, k, h], up)

    def across(b, j, h):
        dd[j, h] = push(b, h, dd_r.at[j, h], sib)

    def both(b, k):
        b1[0, k, 0] = push(b, 0, b1_r.at[0, k, 0], un)
        b1[1, k, 1] = push(b, 1, b1_r.at[1, k, 1], up)
        b1[0, k, 1] = push(b, 1, b1_r.at[0, k, 1], un)
        b1[1, k, 0] = push(b, 0, b1_r.at[1, k, 0], up)
        for h in range(2):
            across(b, k, h)

    for h in range(2):
        a2[h] = push(dp, h, a2_r.at[h], dev(0, 2))
    both(dp, 0)
    upd_ref[...] = upd
    nw_ref[...] = nw
    a1[0, 0].wait_recv()
    a1[0, 1].wait_recv()
    both(wp, 1)
    a1[1, 1].wait_recv()
    a1[1, 0].wait_recv()
    both(wn, 2)

    def onward(k, ww):
        left, right = dev(-1, ww), dev(1, ww)
        b1[0, k, 0].wait_recv()
        b2[0, k] = push(left, 0, b2_r.at[0, k], un)
        b1[1, k, 1].wait_recv()
        b2[1, k] = push(right, 1, b2_r.at[1, k], up)
        across(left, 4 + 2 * k, 0)
        across(right, 5 + 2 * k, 1)
        b1[0, k, 1].wait_recv()
        across(left, 4 + 2 * k, 1)
        b1[1, k, 0].wait_recv()
        across(right, 5 + 2 * k, 0)

    wf = dev(0, 2)
    for h in range(2):
        a2[h].wait_recv()
        spread(wf, 3, h)
        across(wf, 3, h)
    onward(0, 0)
    onward(1, -1)
    onward(2, 1)
    onward(3, 2)
    for k, ww in ((0, 0), (1, -1), (2, 1), (3, 2)):
        for h in range(2):
            b2[h, k].wait_recv()
            across(dev(2, ww), 12 + k, h)
    for cp in dd.values():
        cp.wait_recv()

    for cp in sent:
        cp.wait_send()
    for i, (buf, n) in enumerate(((zr, nz), (pr, NPLANE), (ta, NPLANE), (tb, nz))):
        finish(n, buf, ex_s.at[i])


def store(a, b, c, d, e, ao, bo, co, do, eo, sem):
    rows = e.shape[0] // 8
    pairs = [(e.at[pl.ds(i * rows, rows)], eo.at[pl.ds(i * rows, rows)]) for i in range(8)]
    pairs += [(a, ao), (b, bo), (c, co), (d, do)]
    copies = [pltpu.make_async_copy(i, o, sem.at[n]) for n, (i, o) in enumerate(pairs)]
    for cp in copies:
        cp.start()
    for cp in copies:
        cp.wait()


def body(inputs, query_grad, master_weight, row_factor, col_factor, step):
    T, W = query_grad.shape
    rows = inputs.shape[1]
    nz = lax.axis_size("mp")
    ndp = lax.axis_size("dp")
    H = W // 2
    f32, i16, bf16 = jnp.float32, jnp.int16, jnp.bfloat16
    DMA = pltpu.SemaphoreType.DMA
    hb = (H + 16, 128)
    vm = pl.BlockSpec(memory_space=pltpu.VMEM)
    hbm = pl.BlockSpec(memory_space=pltpu.HBM)
    outs = pl.pallas_call(
        functools.partial(kernel, nz, T * ndp, rows, W * nz),
        out_shape=[
            pltpu.VMEM((128, W), f32),
            pltpu.VMEM((128, W), f32),
            pltpu.VMEM((1, 128), f32),
            pltpu.VMEM((1, W), f32),
            pltpu.VMEM((rows, W), bf16),
        ],
        in_specs=[hbm] * 5 + [pl.BlockSpec(memory_space=pltpu.SMEM)],
        out_specs=[vm, vm, vm, vm, vm],
        scratch_shapes=[
            pltpu.VMEM((128, W), f32),
            pltpu.VMEM((1, 128), f32),
            pltpu.VMEM((1, W), f32),
            DMA((3,)),
            pltpu.VMEM((T, W), bf16),
            pltpu.VMEM((W, T), bf16),
            pltpu.VMEM((16, T, 256), bf16),
            pltpu.VMEM((16, W, 128), f32),
            pltpu.VMEM((4, W, 128), f32),
            pltpu.VMEM((16, 2) + hb, i16),
            pltpu.VMEM((16, 2) + hb, i16),
            pltpu.VMEM((2, 4) + hb, i16),
            pltpu.VMEM((2, 4) + hb, i16),
            pltpu.VMEM((2, 4, 2) + hb, i16),
            pltpu.VMEM((2, 4, 2) + hb, i16),
            pltpu.VMEM((2,) + hb, i16),
            pltpu.VMEM((2,) + hb, i16),
            pltpu.VMEM((2, 2) + hb, i16),
            pltpu.VMEM((2, 2) + hb, i16),
            pltpu.VMEM((nz, 1, 128), f32),
            pltpu.VMEM((NPLANE, 1, W), f32),
            pltpu.VMEM((NPLANE, 1, 128), f32),
            pltpu.VMEM((nz, 1, 128), f32),
            DMA((32,)), DMA, DMA((16,)), DMA((16,)),
            DMA((2, 4)), DMA((2, 4)), DMA((2, 4, 2)), DMA((2, 4, 2)),
            DMA((2,)), DMA((2,)), DMA((2, 2)), DMA((2, 2)),
            DMA((4,)), DMA, DMA, DMA, DMA,
            pltpu.SemaphoreType.REGULAR, pltpu.SemaphoreType.REGULAR,
            DMA((64,)), DMA((2, 2)), DMA((2,)), DMA((2, 4, 2)), DMA((2, 4)), DMA((16, 2)),
        ],
        compiler_params=pltpu.CompilerParams(
            collective_id=0, has_side_effects=True, vmem_limit_bytes=44 * 2**20
        ),
    )(*[
        pltpu.with_memory_space_constraint(a, pltpu.HBM)
        for a in (
            inputs, query_grad, master_weight,
            row_factor.reshape(1, 128), col_factor.reshape(1, W),
        )
    ], step)
    outs = pl.pallas_call(
        store,
        out_shape=[jax.ShapeDtypeStruct(o.shape, o.dtype) for o in outs],
        in_specs=[vm] * 5,
        out_specs=[hbm] * 5,
        scratch_shapes=[DMA((12,))],
        compiler_params=pltpu.CompilerParams(vmem_limit_bytes=8 * 2**20),
    )(*outs)
    return outs[0], outs[1], outs[2].reshape(128), outs[3].reshape(W), outs[4]


def solution(mesh):
    in_specs = (P("dp", None), P("dp", "mp"), P("dp", "mp"), P("dp"), P("mp"), P())
    out_specs = (P("dp", "mp"), P("dp", "mp"), P("dp"), P("mp"), P(None, "mp"))
    return jax.shard_map(body, mesh=mesh, in_specs=in_specs, out_specs=out_specs, check_vma=False)
```

```python
import functools

import jax
import jax.numpy as jnp
from jax import lax
from jax.experimental import pallas as pl
from jax.experimental.pallas import tpu as pltpu
from jax.sharding import PartitionSpec as P

MESH = pl.DeviceIdType.MESH
NX, NY, NC = 4, 4, 2
NPLANE = NX * NY * NC
FAR = (2, 1, 3, 0)
PEAK = 32766.0
TOP = PEAK * PEAK * (1.0 - 1e-4)


def encode(x, buf):
    h = x.shape[0]
    top = jnp.max(jnp.abs(x), axis=0, keepdims=True)
    e = jnp.ceil(jnp.log2(jnp.maximum(top, 1e-30)))
    t = x * (jnp.exp2(-e) * TOP)
    y = t * lax.rsqrt(jnp.maximum(jnp.abs(t), 1e-12))
    buf[0:h, :] = jnp.round(y).astype(jnp.int32).astype(jnp.int16)
    buf[h : h + 16, :] = jnp.broadcast_to(e.astype(jnp.int32), (16, x.shape[1])).astype(jnp.int16)


def decode(buf, h):
    y = buf[0:h, :].astype(jnp.int32).astype(jnp.float32)
    e = buf[h : h + 16, :].astype(jnp.int32).astype(jnp.float32)[0:1, :]
    return y * jnp.abs(y) * (jnp.exp2(e) * (1.0 / TOP))


def kernel(
    nz, total_tokens, total_rows, total_cols,
    x_hbm, q_hbm, mw_hbm, row_hbm, col_hbm, step_ref,
    upd_ref, nw_ref, rown_ref, coln_ref, out_ref,
    mw_ref, row_ref, col_ref, p_sem,
    qcat, qT, X, S, R, sd, rd,
    s1a, r1a, s1b, r1b, s2a, r2a, s2b, r2b,
    zr, pr, ta, tb,
    own_sem, qsem, d_send, d_recv,
    s1a_s, s1a_r, s1b_s, s1b_r, s2a_s, s2a_r, s2b_s, s2b_r,
    ex_s, zr_r, pr_r, ta_r, tb_r, zs1, zs2,
    ag_s, a1_r, a2_r, b1_r, b2_r, dd_r,
):
    T, W = q_hbm.shape
    H = W // 2
    dp = lax.axis_index("dp")
    z = lax.axis_index("mp")
    c = lax.rem(dp, NC)
    cx = lax.div(dp, NY * NC)
    cy = lax.rem(lax.div(dp, NC), NY)
    sib = dp + 1 - 2 * c
    cs = 1 - c
    u = cx * (1 - c) + cy * c
    w = cy * (1 - c) + cx * c
    su = NY * NC - (NY * NC - NC) * c
    sw = NC + (NY * NC - NC) * c
    ru = [lax.rem(u + i, 4) * su for i in range(4)]
    rw = [lax.rem(w + i, 4) * sw for i in range(4)]
    rx = [lax.rem(cx + i, NX) * (NY * NC) for i in range(NX)]
    ry = [lax.rem(cy + i, NY) * NC for i in range(NY)]
    rz = [lax.rem(z + i, nz) for i in range(nz)]

    def dev(i, j):
        return ru[i % 4] + rw[j % 4] + c

    def sdev(i, j):
        return rw[i % 4] + ru[j % 4] + cs

    un, up = dev(1, 0), dev(-1, 0)
    wn, wp = dev(0, 1), dev(0, -1)

    def cols_of(b):
        return pl.ds(pl.multiple_of(b * 128, 128), 128)

    def remote(src, dst, ss, rs, d, zz=None):
        return pltpu.make_async_remote_copy(
            src, dst, ss, rs, device_id=(d, z if zz is None else zz), device_id_type=MESH
        )

    cq = pltpu.make_async_copy(q_hbm, qcat, qsem)
    cq.start()
    loads = {}

    def load(side, p):
        for s in (2 * p, 2 * p + 1):
            o = (FAR[s // 4], FAR[s % 4])
            b = dev(*o) if side else sdev(*o)
            j = 16 * side + s
            cp = pltpu.make_async_copy(
                x_hbm.at[:, cols_of(b)],
                X.at[j // 2, :, pl.ds(128 * (j % 2), 128)],
                own_sem.at[j],
            )
            cp.start()
            loads[j] = cp

    for side, p in ((0, 0), (0, 1)):
        load(side, p)

    bar = pltpu.get_barrier_semaphore()
    zn, zp = rz[1 % nz], rz[nz - 1]
    for d in (sib, un, up, wn, wp):
        pl.semaphore_signal(bar, 1, device_id=(d, z), device_id_type=MESH)
    for zz in (zn, zp):
        pl.semaphore_signal(bar, 1, device_id=(dp, zz), device_id_type=MESH)

    for side, p in (
        (1, 0), (1, 1), (0, 2), (0, 4), (0, 3), (0, 5),
        (1, 2), (1, 4), (1, 3), (1, 5), (0, 6), (0, 7), (1, 6), (1, 7),
    ):
        load(side, p)
    cq.wait()
    qT[...] = qcat[...].T

    cd = {}

    def work(theirs, mine):
        jobs = [8 * 0 + p for p in theirs] + [8 + p for p in mine]
        for j in jobs:
            loads[2 * j].wait()
            loads[2 * j + 1].wait()
        for j in jobs:
            acc = jnp.dot(qT[...], X[j], preferred_element_type=jnp.float32)
            for i in range(2):
                part = acc[:, 128 * i : 128 * i + 128]
                if j >= 8:
                    S[2 * (j - 8) + i] = part
                else:
                    for h in range(2):
                        encode(part[h * H : h * H + H], sd.at[2 * j + i, h])

    def give(*pairs):
        for p in pairs:
            for s in (2 * p, 2 * p + 1):
                cd[s] = remote(sd.at[s], rd.at[s], d_send.at[s], d_recv.at[s], sib)
                cd[s].start()

    def total(*blocks):
        for s in blocks:
            cd[s].wait_recv()
        for s in blocks:
            for h in range(2):
                S[s, h * H : h * H + H, :] = S[s, h * H : h * H + H, :] + decode(rd.at[s, h], H)

    work((0,), ())
    pl.semaphore_wait(bar, 7)
    give(0)
    work((1,), (0, 1))
    give(1)
    params = [
        pltpu.make_async_copy(a, b, p_sem.at[i])
        for i, (a, b) in enumerate(((mw_hbm, mw_ref), (row_hbm, row_ref), (col_hbm, col_ref)))
    ]
    for cp in params:
        cp.start()

    for zz in (zn, zp):
        pl.semaphore_signal(zs1, 1, device_id=(dp, zz), device_id_type=MESH)
    c1a = {}

    def first(*ks):
        total(*ks)
        for k in ks:
            for d in range(2):
                encode(S[k, d * H : d * H + H, :], s1a.at[d, k])
        for k in ks:
            for d, to in ((0, un), (1, up)):
                cp = remote(s1a.at[d, k], r1a.at[d, k], s1a_s.at[d, k], s1a_r.at[d, k], to)
                cp.start()
                c1a[d, k] = cp

    first(0)
    first(1)
    work((2, 4), (2, 4))
    give(2, 4)
    first(2)
    first(3)
    pl.semaphore_wait(zs1, 2)
    for zz in (rz[2 % nz], rz[nz - 2]):
        pl.semaphore_signal(zs2, 1, device_id=(dp, zz), device_id_type=MESH)

    c1b = {}

    def send1b(d, k, h):
        to = un if d == 0 else up
        cp = remote(
            s1b.at[d, k, h], r1b.at[d, k, h], s1b_s.at[d, k, h], s1b_r.at[d, k, h], to
        )
        cp.start()
        c1b[d, k, h] = cp

    def at_once(*ks):
        total(*(4 * g + k for k in ks for g in (1, 2)))
        for k in ks:
            for d in range(2):
                h = 1 - d
                encode(S[4 * (1 + d) + k, h * H : h * H + H, :], s1b.at[d, k, h])
        for k in ks:
            for d in range(2):
                send1b(d, k, 1 - d)

    def with_far(*ks):
        for k in ks:
            for d in range(2):
                c1a[d, k].wait_recv()
        for k in ks:
            for d in range(2):
                encode(
                    S[4 * (1 + d) + k, d * H : d * H + H, :] + decode(r1a.at[d, k], H),
                    s1b.at[d, k, d],
                )
        for k in ks:
            for d in range(2):
                send1b(d, k, d)

    c2a, c2b = {}, {}

    def send2b(d, h):
        to = wn if d == 0 else wp
        cp = remote(s2b.at[d, h], r2b.at[d, h], s2b_s.at[d, h], s2b_r.at[d, h], to)
        cp.start()
        c2b[d, h] = cp

    def gathered(k, *hs):
        for h in hs:
            c1b[0, k, h].wait_recv()
            c1b[1, k, h].wait_recv()
        for h in hs:
            R[k, h * H : h * H + H, :] = (
                S[12 + k, h * H : h * H + H, :]
                + decode(r1b.at[0, k, h], H)
                + decode(r1b.at[1, k, h], H)
            )

    def second(k):
        if k == 0:
            gathered(k, 0, 1)
            for d in range(2):
                encode(R[0, d * H : d * H + H, :], s2a.at[d])
            for d, to in ((0, wn), (1, wp)):
                cp = remote(s2a.at[d], r2a.at[d], s2a_s.at[d], s2a_r.at[d], to)
                cp.start()
                c2a[d] = cp
        else:
            d = k - 1
            gathered(k, 1 - d)
            encode(R[k, (1 - d) * H : (1 - d) * H + H, :], s2b.at[d, 1 - d])
            send2b(d, 1 - d)
            gathered(k, d)

    def second_far(k):
        d = k - 1
        c2a[d].wait_recv()
        encode(R[k, d * H : d * H + H, :] + decode(r2a.at[d], H), s2b.at[d, d])
        send2b(d, d)

    at_once(0)
    with_far(0)
    at_once(1)
    work((3, 5), (3, 5))
    give(3, 5)
    with_far(1)
    at_once(2)
    work((6, 7), (6, 7))
    give(6, 7)
    with_far(2)
    at_once(3)
    with_far(3)
    total(12, 13, 14, 15)
    pl.semaphore_wait(zs2, 2)
    second(0)
    second(1)
    second(2)
    second_far(1)
    second_far(2)
    gathered(3, 0, 1)
    for h in range(2):
        c2b[0, h].wait_recv()
        c2b[1, h].wait_recv()
    for h in range(2):
        R[3, h * H : h * H + H, :] = (
            R[3, h * H : h * H + H, :] + decode(r2b.at[0, h], H) + decode(r2b.at[1, h], H)
        )

    for cp in params:
        cp.wait()
    gT = R[3] * (1.0 / total_tokens)
    zr[pl.ds(z, 1)] = jnp.sum(gT * gT, axis=0, keepdims=True)[None]
    gN = gT.T
    pr[pl.ds(dp, 1)] = jnp.sum(gN * gN, axis=0, keepdims=True)[None]

    far_plane = sorted(
        ((i, j, k) for i in range(NX) for j in range(NY) for k in range(NC) if i or j or k),
        key=lambda o: -(min(o[0], NX - o[0]) + min(o[1], NY - o[1])),
    )
    far_z = sorted(range(1, nz), key=lambda i: -min(i, nz - i))

    def to_plane(buf, ssem, rsem):
        for i, j, k in far_plane:
            peer = rx[i] + ry[j] + (cs if k else c)
            remote(buf.at[pl.ds(dp, 1)], buf.at[pl.ds(dp, 1)], ssem, rsem, peer).start()

    def to_z(buf, ssem, rsem):
        for i in far_z:
            remote(buf.at[pl.ds(z, 1)], buf.at[pl.ds(z, 1)], ssem, rsem, dp, rz[i]).start()

    def finish(n, buf, rsem):
        part = buf.at[pl.ds(0, n - 1)]
        cp = pltpu.make_async_copy(part, part, rsem)
        cp.wait()

    to_z(zr, ex_s.at[0], zr_r)
    to_plane(pr, ex_s.at[1], pr_r)
    mw = mw_ref[...]
    wsum = jnp.sum(mw * mw)
    stepv = jnp.full((1, 128), step_ref[0].astype(jnp.float32), jnp.float32)
    decay = 1.0 - jnp.exp(-0.8 * jnp.log(stepv))
    decay_w = jnp.concatenate([decay] * (W // 128), axis=1)
    finish(nz, zr, zr_r)
    row_new = decay * row_ref[...] + (1.0 - decay) * (jnp.sum(zr[...], axis=0) / total_cols + 1e-30)
    rown_ref[...] = row_new
    half = (gT * lax.rsqrt(row_new)).T
    finish(NPLANE, pr, pr_r)
    col_new = decay_w * col_ref[...] + (1.0 - decay_w) * (
        jnp.sum(pr[...], axis=0) / total_rows + 1e-30
    )
    coln_ref[...] = col_new
    raw = half * lax.rsqrt(col_new)
    rsum = jnp.sum(raw * raw)

    lane = lax.broadcasted_iota(jnp.int32, (1, 1, 128), 2)
    ta[pl.ds(dp, 1)] = jnp.where(lane < 64, rsum, wsum)
    to_plane(ta, ex_s.at[2], ta_r)
    for group in (cd, c1a, c1b, c2a, c2b):
        for cp in group.values():
            cp.wait_send()
    finish(NPLANE, ta, ta_r)
    tb[pl.ds(z, 1)] = jnp.sum(ta[...], axis=0, keepdims=True)
    to_z(tb, ex_s.at[3], tb_r)
    finish(nz, tb, tb_r)
    tot = jnp.sum(tb[...], axis=0) / (total_rows * total_cols)
    clip = jnp.maximum(1.0, jnp.sqrt(tot[:, 0:1]))
    size = 0.01 * jnp.sqrt(tot[:, 64:65] + 1e-06)
    upd = raw * (1.0 / clip)
    nw = mw - size * upd

    def rows_of(b, half=None):
        if half is None:
            return out_ref.at[pl.ds(pl.multiple_of(b * 128, 128), 128)]
        return out_ref.at[pl.ds(pl.multiple_of(b * 128 + half * 64, 64), 64)]

    rows_of(dp)[...] = nw.astype(jnp.bfloat16)

    sent = []

    def push(b, half, rsem, to):
        cp = remote(rows_of(b, half), rows_of(b, half), ag_s.at[len(sent)], rsem, to)
        cp.start()
        sent.append(cp)
        return cp

    a1, a2, b1, b2, dd = {}, {}, {}, {}, {}
    for i in range(2):
        a1[0, i] = push(dp, i, a1_r.at[0, i], wn)
        a1[1, 1 - i] = push(dp, 1 - i, a1_r.at[1, 1 - i], wp)

    def spread(b, k, h):
        b1[0, k, h] = push(b, h, b1_r.at[0, k, h], un)
        b1[1, k, h] = push(b, h, b1_r.at[1, k, h], up)

    def across(b, j, h):
        dd[j, h] = push(b, h, dd_r.at[j, h], sib)

    def both(b, k):
        b1[0, k, 0] = push(b, 0, b1_r.at[0, k, 0], un)
        b1[1, k, 1] = push(b, 1, b1_r.at[1, k, 1], up)
        b1[0, k, 1] = push(b, 1, b1_r.at[0, k, 1], un)
        b1[1, k, 0] = push(b, 0, b1_r.at[1, k, 0], up)
        for h in range(2):
            across(b, k, h)

    for h in range(2):
        a2[h] = push(dp, h, a2_r.at[h], dev(0, 2))
    both(dp, 0)
    upd_ref[...] = upd
    nw_ref[...] = nw
    a1[0, 0].wait_recv()
    a1[0, 1].wait_recv()
    both(wp, 1)
    a1[1, 1].wait_recv()
    a1[1, 0].wait_recv()
    both(wn, 2)

    def onward(k, ww):
        left, right = dev(-1, ww), dev(1, ww)
        b1[0, k, 0].wait_recv()
        b2[0, k] = push(left, 0, b2_r.at[0, k], un)
        b1[1, k, 1].wait_recv()
        b2[1, k] = push(right, 1, b2_r.at[1, k], up)
        across(left, 4 + 2 * k, 0)
        across(right, 5 + 2 * k, 1)
        b1[0, k, 1].wait_recv()
        across(left, 4 + 2 * k, 1)
        b1[1, k, 0].wait_recv()
        across(right, 5 + 2 * k, 0)

    wf = dev(0, 2)
    for h in range(2):
        a2[h].wait_recv()
        spread(wf, 3, h)
        across(wf, 3, h)
    onward(0, 0)
    onward(1, -1)
    onward(2, 1)
    onward(3, 2)
    for k, ww in ((0, 0), (1, -1), (2, 1), (3, 2)):
        for h in range(2):
            b2[h, k].wait_recv()
            across(dev(2, ww), 12 + k, h)
    for cp in dd.values():
        cp.wait_recv()

    for cp in sent:
        cp.wait_send()
    for i, (buf, n) in enumerate(((zr, nz), (pr, NPLANE), (ta, NPLANE), (tb, nz))):
        finish(n, buf, ex_s.at[i])


def store(a, b, c, d, e, ao, bo, co, do, eo, sem):
    rows = e.shape[0] // 8
    pairs = [(e.at[pl.ds(i * rows, rows)], eo.at[pl.ds(i * rows, rows)]) for i in range(8)]
    pairs += [(a, ao), (b, bo), (c, co), (d, do)]
    copies = [pltpu.make_async_copy(i, o, sem.at[n]) for n, (i, o) in enumerate(pairs)]
    for cp in copies:
        cp.start()
    for cp in copies:
        cp.wait()


def body(inputs, query_grad, master_weight, row_factor, col_factor, step):
    T, W = query_grad.shape
    rows = inputs.shape[1]
    nz = lax.axis_size("mp")
    ndp = lax.axis_size("dp")
    H = W // 2
    f32, i16, bf16 = jnp.float32, jnp.int16, jnp.bfloat16
    DMA = pltpu.SemaphoreType.DMA
    hb = (H + 16, 128)
    vm = pl.BlockSpec(memory_space=pltpu.VMEM)
    hbm = pl.BlockSpec(memory_space=pltpu.HBM)
    outs = pl.pallas_call(
        functools.partial(kernel, nz, T * ndp, rows, W * nz),
        out_shape=[
            pltpu.VMEM((128, W), f32),
            pltpu.VMEM((128, W), f32),
            pltpu.VMEM((1, 128), f32),
            pltpu.VMEM((1, W), f32),
            pltpu.VMEM((rows, W), bf16),
        ],
        in_specs=[hbm] * 5 + [pl.BlockSpec(memory_space=pltpu.SMEM)],
        out_specs=[vm, vm, vm, vm, vm],
        scratch_shapes=[
            pltpu.VMEM((128, W), f32),
            pltpu.VMEM((1, 128), f32),
            pltpu.VMEM((1, W), f32),
            DMA((3,)),
            pltpu.VMEM((T, W), bf16),
            pltpu.VMEM((W, T), bf16),
            pltpu.VMEM((16, T, 256), bf16),
            pltpu.VMEM((16, W, 128), f32),
            pltpu.VMEM((4, W, 128), f32),
            pltpu.VMEM((16, 2) + hb, i16),
            pltpu.VMEM((16, 2) + hb, i16),
            pltpu.VMEM((2, 4) + hb, i16),
            pltpu.VMEM((2, 4) + hb, i16),
            pltpu.VMEM((2, 4, 2) + hb, i16),
            pltpu.VMEM((2, 4, 2) + hb, i16),
            pltpu.VMEM((2,) + hb, i16),
            pltpu.VMEM((2,) + hb, i16),
            pltpu.VMEM((2, 2) + hb, i16),
            pltpu.VMEM((2, 2) + hb, i16),
            pltpu.VMEM((nz, 1, 128), f32),
            pltpu.VMEM((NPLANE, 1, W), f32),
            pltpu.VMEM((NPLANE, 1, 128), f32),
            pltpu.VMEM((nz, 1, 128), f32),
            DMA((32,)), DMA, DMA((16,)), DMA((16,)),
            DMA((2, 4)), DMA((2, 4)), DMA((2, 4, 2)), DMA((2, 4, 2)),
            DMA((2,)), DMA((2,)), DMA((2, 2)), DMA((2, 2)),
            DMA((4,)), DMA, DMA, DMA, DMA,
            pltpu.SemaphoreType.REGULAR, pltpu.SemaphoreType.REGULAR,
            DMA((64,)), DMA((2, 2)), DMA((2,)), DMA((2, 4, 2)), DMA((2, 4)), DMA((16, 2)),
        ],
        compiler_params=pltpu.CompilerParams(
            collective_id=0, has_side_effects=True, vmem_limit_bytes=44 * 2**20
        ),
    )(*[
        pltpu.with_memory_space_constraint(a, pltpu.HBM)
        for a in (
            inputs, query_grad, master_weight,
            row_factor.reshape(1, 128), col_factor.reshape(1, W),
        )
    ], step)
    outs = pl.pallas_call(
        store,
        out_shape=[jax.ShapeDtypeStruct(o.shape, o.dtype) for o in outs],
        in_specs=[vm] * 5,
        out_specs=[hbm] * 5,
        scratch_shapes=[DMA((12,))],
        compiler_params=pltpu.CompilerParams(vmem_limit_bytes=8 * 2**20),
    )(*outs)
    return outs[0], outs[1], outs[2].reshape(128), outs[3].reshape(W), outs[4]


def solution(mesh):
    in_specs = (P("dp", None), P("dp", "mp"), P("dp", "mp"), P("dp"), P("mp"), P())
    out_specs = (P("dp", "mp"), P("dp", "mp"), P("dp"), P("mp"), P(None, "mp"))
    return jax.shard_map(body, mesh=mesh, in_specs=in_specs, out_specs=out_specs, check_vma=False)
```

```python
import functools

import jax
import jax.numpy as jnp
from jax import lax
from jax.experimental import pallas as pl
from jax.experimental.pallas import tpu as pltpu
from jax.sharding import PartitionSpec as P

MESH = pl.DeviceIdType.MESH
NX, NY, NC = 4, 4, 2
NPLANE = NX * NY * NC
FAR = (2, 1, 3, 0)
PEAK = 32766.0
TOP = PEAK * PEAK * (1.0 - 1e-4)


def encode(x, buf):
    h = x.shape[0]
    top = jnp.max(jnp.abs(x), axis=0, keepdims=True)
    e = jnp.ceil(jnp.log2(jnp.maximum(top, 1e-30)))
    t = x * (jnp.exp2(-e) * TOP)
    y = t * lax.rsqrt(jnp.maximum(jnp.abs(t), 1e-12))
    buf[0:h, :] = jnp.round(y).astype(jnp.int32).astype(jnp.int16)
    buf[h : h + 16, :] = jnp.broadcast_to(e.astype(jnp.int32), (16, x.shape[1])).astype(jnp.int16)


def decode(buf, h):
    y = buf[0:h, :].astype(jnp.int32).astype(jnp.float32)
    e = buf[h : h + 16, :].astype(jnp.int32).astype(jnp.float32)[0:1, :]
    return y * jnp.abs(y) * (jnp.exp2(e) * (1.0 / TOP))


def kernel(
    nz, total_tokens, total_rows, total_cols,
    x_hbm, q_hbm, mw_hbm, row_hbm, col_hbm, step_ref,
    upd_ref, nw_ref, rown_ref, coln_ref, out_ref,
    mw_ref, row_ref, col_ref, p_sem,
    qcat, qT, X, S, R, sd, rd,
    s1a, r1a, s1b, r1b, s2a, r2a, s2b, r2b,
    zr, pr, ta, tb,
    own_sem, qsem, d_send, d_recv,
    s1a_s, s1a_r, s1b_s, s1b_r, s2a_s, s2a_r, s2b_s, s2b_r,
    ex_s, zr_r, pr_r, ta_r, tb_r, zs1, zs2,
    ag_s, a1_r, a2_r, b1_r, b2_r, dd_r,
):
    T, W = q_hbm.shape
    H = W // 2
    dp = lax.axis_index("dp")
    z = lax.axis_index("mp")
    c = lax.rem(dp, NC)
    cx = lax.div(dp, NY * NC)
    cy = lax.rem(lax.div(dp, NC), NY)
    sib = dp + 1 - 2 * c
    cs = 1 - c
    u = cx * (1 - c) + cy * c
    w = cy * (1 - c) + cx * c
    su = NY * NC - (NY * NC - NC) * c
    sw = NC + (NY * NC - NC) * c
    ru = [lax.rem(u + i, 4) * su for i in range(4)]
    rw = [lax.rem(w + i, 4) * sw for i in range(4)]
    rx = [lax.rem(cx + i, NX) * (NY * NC) for i in range(NX)]
    ry = [lax.rem(cy + i, NY) * NC for i in range(NY)]
    rz = [lax.rem(z + i, nz) for i in range(nz)]

    def dev(i, j):
        return ru[i % 4] + rw[j % 4] + c

    def sdev(i, j):
        return rw[i % 4] + ru[j % 4] + cs

    un, up = dev(1, 0), dev(-1, 0)
    wn, wp = dev(0, 1), dev(0, -1)

    def cols_of(b):
        return pl.ds(pl.multiple_of(b * 128, 128), 128)

    def remote(src, dst, ss, rs, d, zz=None):
        return pltpu.make_async_remote_copy(
            src, dst, ss, rs, device_id=(d, z if zz is None else zz), device_id_type=MESH
        )

    cq = pltpu.make_async_copy(q_hbm, qcat, qsem)
    cq.start()
    loads = {}

    def load(side, p):
        for s in (2 * p, 2 * p + 1):
            o = (FAR[s // 4], FAR[s % 4])
            b = dev(*o) if side else sdev(*o)
            j = 16 * side + s
            cp = pltpu.make_async_copy(
                x_hbm.at[:, cols_of(b)],
                X.at[j // 2, :, pl.ds(128 * (j % 2), 128)],
                own_sem.at[j],
            )
            cp.start()
            loads[j] = cp

    for side, p in ((0, 0), (0, 1)):
        load(side, p)

    bar = pltpu.get_barrier_semaphore()
    zn, zp = rz[1 % nz], rz[nz - 1]
    for d in (sib, un, up, wn, wp):
        pl.semaphore_signal(bar, 1, device_id=(d, z), device_id_type=MESH)
    for zz in (zn, zp):
        pl.semaphore_signal(bar, 1, device_id=(dp, zz), device_id_type=MESH)

    for side, p in (
        (1, 0), (1, 1), (0, 2), (0, 4), (0, 3), (0, 5),
        (1, 2), (1, 4), (1, 3), (1, 5), (0, 6), (0, 7), (1, 6), (1, 7),
    ):
        load(side, p)
    cq.wait()
    qT[...] = qcat[...].T

    cd = {}

    def work(theirs, mine):
        jobs = [8 * 0 + p for p in theirs] + [8 + p for p in mine]
        for j in jobs:
            loads[2 * j].wait()
            loads[2 * j + 1].wait()
        for j in jobs:
            acc = jnp.dot(qT[...], X[j], preferred_element_type=jnp.float32)
            for i in range(2):
                part = acc[:, 128 * i : 128 * i + 128]
                if j >= 8:
                    S[2 * (j - 8) + i] = part
                else:
                    for h in range(2):
                        encode(part[h * H : h * H + H], sd.at[2 * j + i, h])

    def give(*pairs):
        for p in pairs:
            for s in (2 * p, 2 * p + 1):
                cd[s] = remote(sd.at[s], rd.at[s], d_send.at[s], d_recv.at[s], sib)
                cd[s].start()

    def total(*blocks):
        for s in blocks:
            cd[s].wait_recv()
        for s in blocks:
            for h in range(2):
                S[s, h * H : h * H + H, :] = S[s, h * H : h * H + H, :] + decode(rd.at[s, h], H)

    work((0,), ())
    pl.semaphore_wait(bar, 7)
    give(0)
    work((1,), (0, 1))
    give(1)
    params = [
        pltpu.make_async_copy(a, b, p_sem.at[i])
        for i, (a, b) in enumerate(((mw_hbm, mw_ref), (row_hbm, row_ref), (col_hbm, col_ref)))
    ]
    for cp in params:
        cp.start()

    for zz in (zn, zp):
        pl.semaphore_signal(zs1, 1, device_id=(dp, zz), device_id_type=MESH)
    c1a = {}

    def first(*ks):
        total(*ks)
        for k in ks:
            for d in range(2):
                encode(S[k, d * H : d * H + H, :], s1a.at[d, k])
        for k in ks:
            for d, to in ((0, un), (1, up)):
                cp = remote(s1a.at[d, k], r1a.at[d, k], s1a_s.at[d, k], s1a_r.at[d, k], to)
                cp.start()
                c1a[d, k] = cp

    first(0)
    first(1)
    work((2, 4), (2, 4))
    give(2, 4)
    first(2)
    first(3)
    pl.semaphore_wait(zs1, 2)
    for zz in (rz[2 % nz], rz[nz - 2]):
        pl.semaphore_signal(zs2, 1, device_id=(dp, zz), device_id_type=MESH)

    c1b = {}

    def send1b(d, k, h):
        to = un if d == 0 else up
        cp = remote(
            s1b.at[d, k, h], r1b.at[d, k, h], s1b_s.at[d, k, h], s1b_r.at[d, k, h], to
        )
        cp.start()
        c1b[d, k, h] = cp

    def at_once(*ks):
        total(*(4 * g + k for k in ks for g in (1, 2)))
        for k in ks:
            for d in range(2):
                h = 1 - d
                encode(S[4 * (1 + d) + k, h * H : h * H + H, :], s1b.at[d, k, h])
        for k in ks:
            for d in range(2):
                send1b(d, k, 1 - d)

    def with_far(*ks):
        for k in ks:
            for d in range(2):
                c1a[d, k].wait_recv()
        for k in ks:
            for d in range(2):
                encode(
                    S[4 * (1 + d) + k, d * H : d * H + H, :] + decode(r1a.at[d, k], H),
                    s1b.at[d, k, d],
                )
        for k in ks:
            for d in range(2):
                send1b(d, k, d)

    c2a, c2b = {}, {}

    def send2b(d, h):
        to = wn if d == 0 else wp
        cp = remote(s2b.at[d, h], r2b.at[d, h], s2b_s.at[d, h], s2b_r.at[d, h], to)
        cp.start()
        c2b[d, h] = cp

    def gathered(k, *hs):
        for h in hs:
            c1b[0, k, h].wait_recv()
            c1b[1, k, h].wait_recv()
        for h in hs:
            R[k, h * H : h * H + H, :] = (
                S[12 + k, h * H : h * H + H, :]
                + decode(r1b.at[0, k, h], H)
                + decode(r1b.at[1, k, h], H)
            )

    def second(k):
        if k == 0:
            gathered(k, 0, 1)
            for d in range(2):
                encode(R[0, d * H : d * H + H, :], s2a.at[d])
            for d, to in ((0, wn), (1, wp)):
                cp = remote(s2a.at[d], r2a.at[d], s2a_s.at[d], s2a_r.at[d], to)
                cp.start()
                c2a[d] = cp
        else:
            d = k - 1
            gathered(k, 1 - d)
            encode(R[k, (1 - d) * H : (1 - d) * H + H, :], s2b.at[d, 1 - d])
            send2b(d, 1 - d)
            gathered(k, d)

    def second_far(k):
        d = k - 1
        c2a[d].wait_recv()
        encode(R[k, d * H : d * H + H, :] + decode(r2a.at[d], H), s2b.at[d, d])
        send2b(d, d)

    at_once(0)
    with_far(0)
    at_once(1)
    work((3, 5), (3, 5))
    give(3, 5)
    with_far(1)
    work((6, 7), (6, 7))
    give(6, 7)
    at_once(2)
    with_far(2)
    total(12)
    second(0)
    at_once(3)
    with_far(3)
    total(13, 14, 15)
    pl.semaphore_wait(zs2, 2)
    second(1)
    second(2)
    second_far(1)
    second_far(2)
    gathered(3, 0, 1)
    for h in range(2):
        c2b[0, h].wait_recv()
        c2b[1, h].wait_recv()
    for h in range(2):
        R[3, h * H : h * H + H, :] = (
            R[3, h * H : h * H + H, :] + decode(r2b.at[0, h], H) + decode(r2b.at[1, h], H)
        )

    for cp in params:
        cp.wait()
    gT = R[3] * (1.0 / total_tokens)
    zr[pl.ds(z, 1)] = jnp.sum(gT * gT, axis=0, keepdims=True)[None]
    gN = gT.T
    pr[pl.ds(dp, 1)] = jnp.sum(gN * gN, axis=0, keepdims=True)[None]

    far_plane = sorted(
        ((i, j, k) for i in range(NX) for j in range(NY) for k in range(NC) if i or j or k),
        key=lambda o: -(min(o[0], NX - o[0]) + min(o[1], NY - o[1])),
    )
    far_z = sorted(range(1, nz), key=lambda i: -min(i, nz - i))

    def to_plane(buf, ssem, rsem):
        for i, j, k in far_plane:
            peer = rx[i] + ry[j] + (cs if k else c)
            remote(buf.at[pl.ds(dp, 1)], buf.at[pl.ds(dp, 1)], ssem, rsem, peer).start()

    def to_z(buf, ssem, rsem):
        for i in far_z:
            remote(buf.at[pl.ds(z, 1)], buf.at[pl.ds(z, 1)], ssem, rsem, dp, rz[i]).start()

    def finish(n, buf, rsem):
        part = buf.at[pl.ds(0, n - 1)]
        cp = pltpu.make_async_copy(part, part, rsem)
        cp.wait()

    to_z(zr, ex_s.at[0], zr_r)
    to_plane(pr, ex_s.at[1], pr_r)
    mw = mw_ref[...]
    wsum = jnp.sum(mw * mw)
    stepv = jnp.full((1, 128), step_ref[0].astype(jnp.float32), jnp.float32)
    decay = 1.0 - jnp.exp(-0.8 * jnp.log(stepv))
    decay_w = jnp.concatenate([decay] * (W // 128), axis=1)
    finish(nz, zr, zr_r)
    row_new = decay * row_ref[...] + (1.0 - decay) * (jnp.sum(zr[...], axis=0) / total_cols + 1e-30)
    rown_ref[...] = row_new
    half = (gT * lax.rsqrt(row_new)).T
    finish(NPLANE, pr, pr_r)
    col_new = decay_w * col_ref[...] + (1.0 - decay_w) * (
        jnp.sum(pr[...], axis=0) / total_rows + 1e-30
    )
    coln_ref[...] = col_new
    raw = half * lax.rsqrt(col_new)
    rsum = jnp.sum(raw * raw)

    lane = lax.broadcasted_iota(jnp.int32, (1, 1, 128), 2)
    ta[pl.ds(dp, 1)] = jnp.where(lane < 64, rsum, wsum)
    to_plane(ta, ex_s.at[2], ta_r)
    for group in (cd, c1a, c1b, c2a, c2b):
        for cp in group.values():
            cp.wait_send()
    finish(NPLANE, ta, ta_r)
    tb[pl.ds(z, 1)] = jnp.sum(ta[...], axis=0, keepdims=True)
    to_z(tb, ex_s.at[3], tb_r)
    finish(nz, tb, tb_r)
    tot = jnp.sum(tb[...], axis=0) / (total_rows * total_cols)
    clip = jnp.maximum(1.0, jnp.sqrt(tot[:, 0:1]))
    size = 0.01 * jnp.sqrt(tot[:, 64:65] + 1e-06)
    upd = raw * (1.0 / clip)
    nw = mw - size * upd

    def rows_of(b, half=None):
        if half is None:
            return out_ref.at[pl.ds(pl.multiple_of(b * 128, 128), 128)]
        return out_ref.at[pl.ds(pl.multiple_of(b * 128 + half * 64, 64), 64)]

    rows_of(dp)[...] = nw.astype(jnp.bfloat16)

    sent = []

    def push(b, half, rsem, to):
        cp = remote(rows_of(b, half), rows_of(b, half), ag_s.at[len(sent)], rsem, to)
        cp.start()
        sent.append(cp)
        return cp

    a1, a2, b1, b2, dd = {}, {}, {}, {}, {}
    for i in range(2):
        a1[0, i] = push(dp, i, a1_r.at[0, i], wn)
        a1[1, 1 - i] = push(dp, 1 - i, a1_r.at[1, 1 - i], wp)

    def spread(b, k, h):
        b1[0, k, h] = push(b, h, b1_r.at[0, k, h], un)
        b1[1, k, h] = push(b, h, b1_r.at[1, k, h], up)

    def across(b, j, h):
        dd[j, h] = push(b, h, dd_r.at[j, h], sib)

    def both(b, k):
        b1[0, k, 0] = push(b, 0, b1_r.at[0, k, 0], un)
        b1[1, k, 1] = push(b, 1, b1_r.at[1, k, 1], up)
        b1[0, k, 1] = push(b, 1, b1_r.at[0, k, 1], un)
        b1[1, k, 0] = push(b, 0, b1_r.at[1, k, 0], up)
        for h in range(2):
            across(b, k, h)

    for h in range(2):
        a2[h] = push(dp, h, a2_r.at[h], dev(0, 2))
    both(dp, 0)
    upd_ref[...] = upd
    nw_ref[...] = nw
    a1[0, 0].wait_recv()
    a1[0, 1].wait_recv()
    both(wp, 1)
    a1[1, 1].wait_recv()
    a1[1, 0].wait_recv()
    both(wn, 2)

    def onward(k, ww):
        left, right = dev(-1, ww), dev(1, ww)
        b1[0, k, 0].wait_recv()
        b2[0, k] = push(left, 0, b2_r.at[0, k], un)
        b1[1, k, 1].wait_recv()
        b2[1, k] = push(right, 1, b2_r.at[1, k], up)
        across(left, 4 + 2 * k, 0)
        across(right, 5 + 2 * k, 1)
        b1[0, k, 1].wait_recv()
        across(left, 4 + 2 * k, 1)
        b1[1, k, 0].wait_recv()
        across(right, 5 + 2 * k, 0)

    wf = dev(0, 2)
    for h in range(2):
        a2[h].wait_recv()
        spread(wf, 3, h)
        across(wf, 3, h)
    onward(0, 0)
    onward(1, -1)
    onward(2, 1)
    onward(3, 2)
    for k, ww in ((0, 0), (1, -1), (2, 1), (3, 2)):
        for h in range(2):
            b2[h, k].wait_recv()
            across(dev(2, ww), 12 + k, h)
    for cp in dd.values():
        cp.wait_recv()

    for cp in sent:
        cp.wait_send()
    for i, (buf, n) in enumerate(((zr, nz), (pr, NPLANE), (ta, NPLANE), (tb, nz))):
        finish(n, buf, ex_s.at[i])


def store(a, b, c, d, e, ao, bo, co, do, eo, sem):
    rows = e.shape[0] // 8
    pairs = [(e.at[pl.ds(i * rows, rows)], eo.at[pl.ds(i * rows, rows)]) for i in range(8)]
    pairs += [(a, ao), (b, bo), (c, co), (d, do)]
    copies = [pltpu.make_async_copy(i, o, sem.at[n]) for n, (i, o) in enumerate(pairs)]
    for cp in copies:
        cp.start()
    for cp in copies:
        cp.wait()


def body(inputs, query_grad, master_weight, row_factor, col_factor, step):
    T, W = query_grad.shape
    rows = inputs.shape[1]
    nz = lax.axis_size("mp")
    ndp = lax.axis_size("dp")
    H = W // 2
    f32, i16, bf16 = jnp.float32, jnp.int16, jnp.bfloat16
    DMA = pltpu.SemaphoreType.DMA
    hb = (H + 16, 128)
    vm = pl.BlockSpec(memory_space=pltpu.VMEM)
    hbm = pl.BlockSpec(memory_space=pltpu.HBM)
    outs = pl.pallas_call(
        functools.partial(kernel, nz, T * ndp, rows, W * nz),
        out_shape=[
            pltpu.VMEM((128, W), f32),
            pltpu.VMEM((128, W), f32),
            pltpu.VMEM((1, 128), f32),
            pltpu.VMEM((1, W), f32),
            pltpu.VMEM((rows, W), bf16),
        ],
        in_specs=[hbm] * 5 + [pl.BlockSpec(memory_space=pltpu.SMEM)],
        out_specs=[vm, vm, vm, vm, vm],
        scratch_shapes=[
            pltpu.VMEM((128, W), f32),
            pltpu.VMEM((1, 128), f32),
            pltpu.VMEM((1, W), f32),
            DMA((3,)),
            pltpu.VMEM((T, W), bf16),
            pltpu.VMEM((W, T), bf16),
            pltpu.VMEM((16, T, 256), bf16),
            pltpu.VMEM((16, W, 128), f32),
            pltpu.VMEM((4, W, 128), f32),
            pltpu.VMEM((16, 2) + hb, i16),
            pltpu.VMEM((16, 2) + hb, i16),
            pltpu.VMEM((2, 4) + hb, i16),
            pltpu.VMEM((2, 4) + hb, i16),
            pltpu.VMEM((2, 4, 2) + hb, i16),
            pltpu.VMEM((2, 4, 2) + hb, i16),
            pltpu.VMEM((2,) + hb, i16),
            pltpu.VMEM((2,) + hb, i16),
            pltpu.VMEM((2, 2) + hb, i16),
            pltpu.VMEM((2, 2) + hb, i16),
            pltpu.VMEM((nz, 1, 128), f32),
            pltpu.VMEM((NPLANE, 1, W), f32),
            pltpu.VMEM((NPLANE, 1, 128), f32),
            pltpu.VMEM((nz, 1, 128), f32),
            DMA((32,)), DMA, DMA((16,)), DMA((16,)),
            DMA((2, 4)), DMA((2, 4)), DMA((2, 4, 2)), DMA((2, 4, 2)),
            DMA((2,)), DMA((2,)), DMA((2, 2)), DMA((2, 2)),
            DMA((4,)), DMA, DMA, DMA, DMA,
            pltpu.SemaphoreType.REGULAR, pltpu.SemaphoreType.REGULAR,
            DMA((64,)), DMA((2, 2)), DMA((2,)), DMA((2, 4, 2)), DMA((2, 4)), DMA((16, 2)),
        ],
        compiler_params=pltpu.CompilerParams(
            collective_id=0, has_side_effects=True, vmem_limit_bytes=44 * 2**20
        ),
    )(*[
        pltpu.with_memory_space_constraint(a, pltpu.HBM)
        for a in (
            inputs, query_grad, master_weight,
            row_factor.reshape(1, 128), col_factor.reshape(1, W),
        )
    ], step)
    outs = pl.pallas_call(
        store,
        out_shape=[jax.ShapeDtypeStruct(o.shape, o.dtype) for o in outs],
        in_specs=[vm] * 5,
        out_specs=[hbm] * 5,
        scratch_shapes=[DMA((12,))],
        compiler_params=pltpu.CompilerParams(vmem_limit_bytes=8 * 2**20),
    )(*outs)
    return outs[0], outs[1], outs[2].reshape(128), outs[3].reshape(W), outs[4]


def solution(mesh):
    in_specs = (P("dp", None), P("dp", "mp"), P("dp", "mp"), P("dp"), P("mp"), P())
    out_specs = (P("dp", "mp"), P("dp", "mp"), P("dp"), P("mp"), P(None, "mp"))
    return jax.shard_map(body, mesh=mesh, in_specs=in_specs, out_specs=out_specs, check_vma=False)
```
